128 devices in a mesh: seq: 16 (over x, z), dp: 8 (over y, core).
Axes of the slice: x: 4, y: 4, z: 4, core: 2. Of those that a mesh axis runs over, the one named last changes fastest.
Arguments:
- tokens: bfloat16 [8, 8192, 1280], P('dp', 'seq'), may hold values from -10 to 10
- queries: bfloat16 [1024, 1280], replicated, may hold values from -400 to 400
- key_weight: bfloat16 [1280, 1280], replicated, may hold values from -0.15625 to 0.15625
- value_weight: bfloat16 [1280, 1280], replicated, may hold values from -0.15625 to 0.15625
- out_grad: bfloat16 [8, 1024, 1280], P('dp'), may hold values from -6 to 6
Outputs:
- attended: bfloat16 [8, 1024, 1280], P('dp')
- query_grad: float32 [1024, 1280], replicated
- key_wgrad: float32 [1280, 1280], P(('seq', 'dp'))
- value_wgrad: float32 [1280, 1280], P(('seq', 'dp'))
The draws below stay inside these ranges and needn't reach their ends.
All inputs are finite; a program needn't handle non-finite values.
Results may differ from the reference program's by a relative error of at most 0.035.
The reference program's roundings to bfloat16 on the way (of `normed`, `weights`, `vgrad`, `sgrad` and `kgrad`) count: a program that leaves them out, or rounds other values in their place, can miss the bound.
Values sent between devices are 32-bit elements; how exact they have to be, the bound alone decides.
No kernel may reach another device: no remote copies, remote signals or barrier semaphores. Data moves between devices by JAX's collectives and lax.ppermute only.
A program may use at most 512 MiB of HBM per device.

```python
import jax
import jax.numpy as jnp
from jax import lax

C = 1280
H = 10
HD = 128
L = 1024
TOK_DEV = 512
D = 1280
SEQLEN = 8192
BATCH = 8


def draw_tokens(key, part):
    key = jax.random.fold_in(key, 11)
    first, second = jax.random.split(key, 2)
    half = TOK_DEV // 2
    noise = jax.random.normal(first, (BATCH, SEQLEN, C), jnp.float32)
    region = jax.random.normal(second, (BATCH, SEQLEN // half, C), jnp.float32)
    region = jnp.repeat(region, half, axis=1)
    mixed = noise + 1.5 * region
    return jnp.clip(mixed, -10.0, 10.0).astype(jnp.bfloat16)


def draw_queries(key, part):
    key = jax.random.fold_in(key, 23)
    first = jax.random.fold_in(key, 0)
    base = jax.random.normal(first, (L, H, HD), jnp.float32)
    return jnp.clip(base, -400.0, 400.0).reshape(L, H * HD).astype(jnp.bfloat16)


def shard_levels(stream_key, extent, cuts, least, largest):
    loudness = 1.0
    for axis_at, shards_of in cuts:
        heights = jax.random.uniform(jax.random.fold_in(jax.random.fold_in(stream_key, 6), axis_at), (shards_of,), jnp.float32, least / len(cuts), largest / len(cuts))
        loudness = loudness * jnp.repeat(jnp.exp(heights), extent[axis_at] // shards_of).reshape((-1,) + (1,) * (len(extent) - 1 - axis_at))
    return loudness


def centred(stream_key, dims, deviation, bound, cuts=(), dtype=jnp.bfloat16):
    entries = jax.random.normal(stream_key, dims, jnp.float32) * deviation
    if len(cuts) > 0:
        entries = shard_levels(stream_key, dims, cuts, -0.22, 0.18) * entries
    return jnp.clip(entries, min=-bound, max=bound).astype(dtype)


def setup_inputs(seed: int = 0) -> dict:
    streams_of = jax.random.split(jax.random.key(seed), 6)
    tokens = draw_tokens(jax.random.fold_in(streams_of[5], 71), 0)
    queries = draw_queries(jax.random.fold_in(streams_of[5], 71), 0)
    key_weight = centred(streams_of[2], (C, D), C ** -0.5, 0.15625)
    value_weight = centred(streams_of[3], (C, D), C ** -0.5, 0.15625)
    out_grad = centred(streams_of[4], (BATCH, L, D), 1.0, 6.0, ((0, 8),))
    return dict(tokens=tokens, queries=queries, key_weight=key_weight, value_weight=value_weight, out_grad=out_grad)


def layer_norm(rows):
    values = rows.astype(jnp.float32)
    centre = values - lax.optimization_barrier(jnp.mean(values, axis=-1, keepdims=True))
    spread = lax.optimization_barrier(jnp.mean(centre * centre, axis=-1, keepdims=True))
    return (centre * lax.rsqrt(spread + 1e-05)).astype(jnp.bfloat16)

def reference(tokens, queries, key_weight, value_weight, out_grad):
    scale = HD ** (-0.5)
    blocks = SEQLEN // TOK_DEV
    query_heads = queries.reshape(L, H, HD).astype(jnp.float32)
    outs = []
    query_grad = jnp.zeros((L, D), jnp.float32)
    key_wgrad = jnp.zeros((C, D), jnp.float32)
    value_wgrad = jnp.zeros((C, D), jnp.float32)
    for sample in range(BATCH):
        normed = layer_norm(tokens[sample])
        keys = jnp.dot(normed, key_weight, preferred_element_type=jnp.float32).astype(jnp.bfloat16)
        vals = jnp.dot(normed, value_weight, preferred_element_type=jnp.float32).astype(jnp.bfloat16)
        key_heads = keys.reshape(SEQLEN, H, HD).astype(jnp.float32)
        val_heads = vals.reshape(SEQLEN, H, HD).astype(jnp.float32)
        scores = jnp.einsum('lhd,thd->hlt', query_heads, key_heads) * scale
        split = scores.reshape(H, L, blocks, TOK_DEV)
        block_top = lax.optimization_barrier(jnp.max(split, axis=3))
        shifted = jnp.exp(split - block_top[..., None])
        block_total = lax.optimization_barrier(jnp.sum(shifted, axis=3))
        weights = shifted.astype(jnp.bfloat16).astype(jnp.float32)
        block_numer = jnp.einsum('hlnt,nthd->lhnd', weights, val_heads.reshape(blocks, TOK_DEV, H, HD))
        top = lax.optimization_barrier(jnp.max(block_top, axis=2))
        factor = jnp.exp(block_top - top[..., None])
        total = lax.optimization_barrier(jnp.sum(block_total * factor, axis=2))
        numer = lax.optimization_barrier(jnp.sum(block_numer * jnp.transpose(factor, (1, 0, 2))[..., None], axis=2))
        attended = (numer / jnp.transpose(total)[..., None]).astype(jnp.bfloat16)
        outs.append(attended.reshape(L, D))
        lse = top + jnp.log(total)
        probs = jnp.exp(scores - lse[..., None])
        grad_heads = out_grad[sample].reshape(L, H, HD).astype(jnp.float32)
        delta = jnp.transpose(lax.optimization_barrier(jnp.sum(grad_heads * attended.astype(jnp.float32), axis=2)))
        probs_low = probs.astype(jnp.bfloat16).astype(jnp.float32)
        vgrad = jnp.einsum('hlt,lhd->thd', probs_low, grad_heads).astype(jnp.bfloat16)
        pgrad = jnp.einsum('lhd,thd->hlt', grad_heads, val_heads)
        sgrad = (probs * (pgrad - delta[..., None]) * scale).astype(jnp.bfloat16).astype(jnp.float32)
        query_grad = query_grad + jnp.einsum('hlt,thd->lhd', sgrad, key_heads).reshape(L, D)
        kgrad = jnp.einsum('hlt,lhd->thd', sgrad, query_heads).astype(jnp.bfloat16)
        key_wgrad = key_wgrad + jnp.dot(normed.T, kgrad.reshape(SEQLEN, D), preferred_element_type=jnp.float32)
        value_wgrad = value_wgrad + jnp.dot(normed.T, vgrad.reshape(SEQLEN, D), preferred_element_type=jnp.float32)
    return (jnp.stack(outs), query_grad, key_wgrad, value_wgrad)
```

```python
import functools

import jax
import jax.numpy as jnp
import numpy as np
from jax import lax
from jax.experimental import pallas as pl
from jax.experimental.pallas import tpu as pltpu
from jax.sharding import PartitionSpec as P

H = 10
HD = 128
T = 512
L = 1024
D = 1280
PAIR = 2 * HD
SCALE = HD ** (-0.5)
VMEM_LIMIT = 56 * 1024 * 1024
PARTS = (((0, 1, 2), ("y", "x", "z")), ((3, 4), ("z", "y", "x")))
F32 = jnp.float32
BF16 = jnp.bfloat16


def shift(array, axis, step):
    if axis == "x":
        return lax.ppermute(array, "seq", [(a * 4 + b, (a + step) % 4 * 4 + b) for a in range(4) for b in range(4)])
    if axis == "z":
        return lax.ppermute(array, "seq", [(a * 4 + b, a * 4 + (b + step) % 4) for a in range(4) for b in range(4)])
    if axis == "y":
        return lax.ppermute(array, "dp", [(a * 2 + b, (a + step) % 4 * 2 + b) for a in range(4) for b in range(2)])
    return lax.ppermute(array, "dp", [(a * 2 + b, a * 2 + 1 - b) for a in range(4) for b in range(2)])


def nt_dot(a, b):
    return lax.dot_general(a, b, (((1,), (1,)), ((), ())), preferred_element_type=F32)


def dot(a, b):
    return jnp.dot(a, b, preferred_element_type=F32)


def params():
    return pltpu.CompilerParams(vmem_limit_bytes=VMEM_LIMIT)


def cost(flops, moved):
    return pl.CostEstimate(flops=int(flops), bytes_accessed=int(moved), transcendentals=0)


def full(shape):
    return pl.BlockSpec(shape, lambda *_: (0,) * len(shape))


SMEM = pl.BlockSpec(memory_space=pltpu.SMEM)


def forward_kernel(place, tok, kw, vw, q, g, k_out, v_out, normed_out, n0, n1, n2, n3, stats, normed, s, w, numer):
    @pl.when(pl.program_id(0) == 0)
    def _():
        values = tok[...].astype(F32)
        centre = values - jnp.mean(values, axis=-1, keepdims=True)
        spread = jnp.mean(centre * centre, axis=-1, keepdims=True)
        normed[...] = (centre * lax.rsqrt(spread + 1e-05)).astype(BF16)
        normed_out[...] = normed[...]

    keys = dot(normed[...], kw[...]).astype(BF16)
    vals = dot(normed[...], vw[...]).astype(BF16)
    k_out[...] = keys
    v_out[...] = vals
    vals_t = vals.T
    grad_t = g[...].T
    for j in range(2):
        head = slice(j * HD, (j + 1) * HD)
        s[j] = nt_dot(keys[:, head], q[:, head])
        for tile in range(L // 128):
            at = slice(tile * 128, (tile + 1) * 128)
            scores = s[j, :, at] * SCALE
            high = jnp.max(scores, axis=0, keepdims=True)
            shifted = jnp.exp(scores - high)
            stats[0, j : j + 1, at] = high
            stats[0, 2 + j : 3 + j, at] = jnp.sum(shifted, axis=0, keepdims=True)
            w[j, :, at] = shifted.astype(BF16)
        part = dot(vals_t[head, :], w[j])
        numer[head, :] = part
        stats[0, 4 + j : 5 + j, :] = jnp.sum(part * grad_t[head, :].astype(F32), axis=0, keepdims=True)
    stats[0, 6:8, :] = jnp.zeros((2, L), F32)
    for k, out in enumerate((n0, n1, n2, n3)):
        start = pl.multiple_of(lax.rem(place[0] + k, 4) * 256, 256)
        out[...] = numer[:, pl.ds(start, 256)]


def forward(place, tokens, kw, vw, q, g):
    cols = lambda rows: pl.BlockSpec((rows, PAIR), lambda i: (0, i))
    return pl.pallas_call(
        forward_kernel,
        grid=(H // 2,),
        in_specs=[SMEM, full((T, D)), cols(D), cols(D), cols(L), cols(L)],
        out_specs=[cols(T), cols(T), full((T, D))]
        + [pl.BlockSpec((PAIR, 256), lambda i: (i, 0))] * 4
        + [pl.BlockSpec((1, 8, L), lambda i: (i, 0, 0))],
        out_shape=[jax.ShapeDtypeStruct((T, D), BF16)] * 3
        + [jax.ShapeDtypeStruct((D, 256), F32)] * 4
        + [jax.ShapeDtypeStruct((H // 2, 8, L), F32)],
        scratch_shapes=[
            pltpu.VMEM((T, D), BF16),
            pltpu.VMEM((2, T, L), F32),
            pltpu.VMEM((2, T, L), BF16),
            pltpu.VMEM((PAIR, L), F32),
        ],
        compiler_params=params(),
        cost_estimate=cost(1.2e10, 2.4e7),
        name="forward",
    )(place, tokens, kw, vw, q, g)


def merge(blocks):
    top = functools.reduce(jnp.maximum, [b[:, 0:2, :] for b in blocks])
    total = jnp.zeros_like(top)
    inner = jnp.zeros_like(top)
    for b in blocks:
        factor = jnp.exp(b[:, 0:2, :] - top)
        total += b[:, 2:4, :] * factor
        inner += b[:, 4:6, :] * factor
    return top, total, inner


def merge_kernel(s0, s1, s2, s3, out):
    top, total, inner = merge((s0, s1, s2, s3))
    out[:, 0:2, :] = top
    out[:, 2:4, :] = total
    out[:, 4:6, :] = inner
    out[:, 6:8, :] = jnp.zeros_like(top)


def finish_kernel(s0, s1, s2, s3, out):
    top, total, inner = merge((s0, s1, s2, s3))
    out[:, 0:2, :] = top + jnp.log(total)
    out[:, 2:4, :] = inner / total
    out[:, 4:6, :] = total
    out[:, 6:8, :] = top


def merged(kernel, blocks, name):
    return pl.pallas_call(
        kernel,
        out_shape=jax.ShapeDtypeStruct((H // 2, 8, L), F32),
        compiler_params=params(),
        cost_estimate=cost(1e6, 8e5),
        name=name,
    )(*blocks)


def reorder_kernel(order, normed, out):
    feature = lax.broadcasted_iota(jnp.int32, (D, D), 0)
    choose = jnp.where(feature == order[...], 1.0, 0.0).astype(BF16)
    out[...] = dot(normed[...], choose).astype(BF16).T


def reorder(order, normed):
    return pl.pallas_call(
        reorder_kernel,
        out_shape=jax.ShapeDtypeStruct((D, T), BF16),
        compiler_params=params(),
        cost_estimate=cost(2 * T * D * D, 3e6),
        name="reorder",
    )(order, normed)


def row_order(place, axes):
    digits = np.indices((2, 4, 4, 4, 10)).reshape(5, D)
    own = dict(x=place[0], z=place[1], y=place[2])
    spot = {a: (own[a] + jnp.asarray(digits[1 + i], jnp.int32)) % 4 for i, a in enumerate(axes)}
    core = (place[3] + jnp.asarray(digits[0], jnp.int32)) % 2
    owner = ((spot["x"] * 4 + spot["z"]) * 4 + spot["y"]) * 2 + core
    return (owner * 10 + jnp.asarray(digits[4], jnp.int32)).reshape(1, D)


def backward_kernel(place, nt, keys, vals, q, g, fin, mine, theirs, s, pg, p, sg, query):
    grads = []
    keys_t = keys[...].T
    for j in range(2):
        head = slice(j * HD, (j + 1) * HD)
        s[j] = nt_dot(keys[:, head], q[:, head])
        pg[j] = nt_dot(vals[:, head], g[:, head])
        for tile in range(L // 128):
            at = slice(tile * 128, (tile + 1) * 128)
            probs = jnp.exp(s[j, :, at] * SCALE - fin[0, j : j + 1, at])
            p[j, :, at] = probs.astype(BF16)
            sg[j, :, at] = (probs * (pg[j, :, at] - fin[0, 2 + j : 3 + j, at]) * SCALE).astype(BF16)
        vgrad = dot(p[j], g[:, head]).astype(BF16)
        kgrad = dot(sg[j], q[:, head]).astype(BF16)
        query[:, head] = dot(keys_t[head, :], sg[j]).T
        grads.append((kgrad, vgrad))
    key_rows = dot(nt[...], jnp.concatenate([grads[0][0], grads[1][0]], axis=1))
    value_rows = dot(nt[...], jnp.concatenate([grads[0][1], grads[1][1]], axis=1))
    for half, out in enumerate((mine, theirs)):
        for k in range(4):
            rows = slice(half * 640 + k * 160, half * 640 + (k + 1) * 160)
            out[k, 0:160, :] = key_rows[rows]
            out[k, 160:320, :] = value_rows[rows]
            start = lax.rem(place[0] + half, 2) * 512 + lax.rem(place[1] + k, 4) * 128
            out[k, 320:448, :] = query[pl.ds(pl.multiple_of(start, 128), 128), :]


def backward(place, nt, keys, vals, q, g, fin, pairs):
    first, width = pairs[0], len(pairs) * PAIR
    cols = lambda rows: pl.BlockSpec((rows, PAIR), lambda i: (0, i + first))
    out = pl.BlockSpec((4, 448, PAIR), lambda i: (0, 0, i))
    return pl.pallas_call(
        backward_kernel,
        grid=(len(pairs),),
        in_specs=[SMEM, full((D, T)), cols(T), cols(T), cols(L), cols(L), pl.BlockSpec((1, 8, L), lambda i: (i + first, 0, 0))],
        out_specs=[out, out],
        out_shape=[jax.ShapeDtypeStruct((4, 448, width), F32)] * 2,
        scratch_shapes=[
            pltpu.VMEM((2, T, L), F32),
            pltpu.VMEM((2, T, L), F32),
            pltpu.VMEM((2, T, L), BF16),
            pltpu.VMEM((2, T, L), BF16),
            pltpu.VMEM((L, PAIR), F32),
        ],
        compiler_params=params(),
        cost_estimate=cost(3.2e9 * len(pairs), 4e6 * len(pairs)),
        name="backward",
    )(place, nt, keys, vals, q, g, fin)


def by_columns(kernel, ins, out_rows, name):
    width = ins[0].shape[-1]
    spec = lambda shape: pl.BlockSpec(shape[:-1] + (PAIR,), lambda i, n=len(shape): (0,) * (n - 1) + (i,))
    outs = [(rows, width) for rows in out_rows]
    return pl.pallas_call(
        kernel,
        grid=(width // PAIR,),
        in_specs=[spec(a.shape) for a in ins],
        out_specs=[spec(o) for o in outs],
        out_shape=[jax.ShapeDtypeStruct(o, F32) for o in outs],
        compiler_params=params(),
        cost_estimate=cost(1e6, 4 * (sum(a.size for a in ins) + sum(r for r in out_rows) * width)),
        name=name,
    )(*ins)


def pair_kernel(mine, other, *outs):
    for k, out in enumerate(outs):
        out[...] = mine[k] + other[k]


def four(a0, a1, a2, a3):
    return (a0[...] + a2[...]) + (a1[...] + a3[...])


def second_kernel(a0, a1, a2, a3, *outs):
    rows = four(a0, a1, a2, a3)
    for k, out in enumerate(outs):
        out[0:40, :] = rows[k * 40 : (k + 1) * 40]
        out[40:80, :] = rows[160 + k * 40 : 160 + (k + 1) * 40]
        out[80:208, :] = rows[320:448]


def third_kernel(a0, a1, a2, a3, *outs):
    rows = four(a0, a1, a2, a3)
    for k, out in enumerate(outs):
        out[0:128, :] = rows[80:208]
        out[128:138, :] = rows[k * 10 : (k + 1) * 10]
        out[138:148, :] = rows[40 + k * 10 : 40 + (k + 1) * 10]
        out[148:152, :] = jnp.zeros((4, PAIR), F32)


def last_kernel(a0, a1, a2, a3, query, key_rows, value_rows):
    rows = four(a0, a1, a2, a3)
    query[...] = rows[0:128]
    key_rows[...] = rows[128:138]
    value_rows[...] = rows[138:148]


def exchange(chunks, axis):
    far = {k: shift(chunks[k], axis, k) for k in (2, 1, 3)}
    return [chunks[0], far[1], far[2], far[3]]


def place_query_kernel(place, own, other, out):
    at = 0
    for i, (pairs, axes) in enumerate(PARTS):
        cols = slice(at, at + len(pairs) * PAIR)
        at = cols.stop
        for k in range(4):
            block = lax.rem(place[1 + i] + 4 - k, 4) * 128
            start = pl.multiple_of(place[0] * 512 + block, 128)
            out[pl.ds(start, 128), cols] = own[k, :, cols]
            start = pl.multiple_of((1 - place[0]) * 512 + block, 128)
            out[pl.ds(start, 128), cols] = other[k, :, cols]


def numer_x_kernel(place, n0, n1, n2, n3, s0, s1, s2, s3, fin, z0, z1, z2, z3, total):
    at = pl.ds(pl.multiple_of(place[0] * 256, 256), 256)
    for h in range(H):
        rows = slice(h * HD, (h + 1) * HD)
        pair, j = h // 2, h % 2
        top = fin[pair, 6 + j : 7 + j, at]
        acc = jnp.zeros((HD, 256), F32)
        for n, s in ((n0, s0), (n1, s1), (n2, s2), (n3, s3)):
            acc += n[rows, :] * jnp.exp(s[pair, j : j + 1, at] - top)
        total[rows, :] = acc
    for k, out in enumerate((z0, z1, z2, z3)):
        spot = lax.rem(place[1] + k, 4)
        row = pl.multiple_of(lax.rem(spot, 2) * 640, 640)
        lane = pl.multiple_of(lax.div(spot, 2) * 128, 128)
        out[...] = total[pl.ds(row, 640), pl.ds(lane, 128)]


def numer_z_kernel(place, z0, z1, z2, z3, fin, out):
    spot = place[1]
    at = pl.ds(pl.multiple_of(place[0] * 256 + lax.div(spot, 2) * 128, 128), 128)
    upper = lax.rem(spot, 2) == 1
    rows = four(z0, z1, z2, z3)
    for h in range(5):
        low = fin[h // 2, 4 + h % 2 : 5 + h % 2, at]
        high = fin[(5 + h) // 2, 4 + (5 + h) % 2 : 5 + (5 + h) % 2, at]
        total = jnp.where(upper, high, low)
        out[:, h * HD : (h + 1) * HD] = (rows[h * HD : (h + 1) * HD] / total).T


def round_kernel(x, out):
    out[...] = x[0].astype(BF16)


def on_device(tokens, queries, key_weight, value_weight, out_grad):
    seq, dp = lax.axis_index("seq"), lax.axis_index("dp")
    place = jnp.stack([seq // 4, seq % 4, dp // 2, dp % 2]).astype(jnp.int32)
    own = dict(x=place[0], z=place[1], y=place[2])
    core = place[3]
    grad = out_grad[0]
    vmem = pl.BlockSpec(memory_space=pltpu.VMEM)

    keys, vals, normed, n0, n1, n2, n3, stats = forward(place, tokens[0], key_weight, value_weight, queries, grad)
    near = exchange([stats] * 4, "x")
    numer = exchange([n0, n1, n2, n3], "x")
    orders = [reorder(row_order(place, axes), normed) for _, axes in PARTS]
    group = merged(merge_kernel, near, "merge")
    fin = merged(finish_kernel, exchange([group] * 4, "z"), "finish")

    sums = []
    for (pairs, axes), nt in zip(PARTS, orders):
        mine, theirs = backward(jnp.stack([core, own[axes[0]]]), nt, keys, vals, queries, grad, fin, pairs)
        other = shift(theirs, "c", 1)
        chunks = by_columns(pair_kernel, [mine, other], [448] * 4, "pair")
        sums.append(exchange(chunks, axes[0]))

    zs = pl.pallas_call(
        numer_x_kernel,
        in_specs=[SMEM] + [vmem] * 9,
        out_shape=[jax.ShapeDtypeStruct((640, 128), F32)] * 4,
        scratch_shapes=[pltpu.VMEM((D, 256), F32)],
        compiler_params=params(),
        cost_estimate=cost(1e7, 7e6),
        name="numer_x",
    )(place, *numer, *near, fin)
    share = pl.pallas_call(
        numer_z_kernel,
        in_specs=[SMEM] + [vmem] * 5,
        out_shape=jax.ShapeDtypeStruct((128, 640), F32),
        compiler_params=params(),
        cost_estimate=cost(1e6, 2e6),
        name="numer_z",
    )(place, *exchange(zs, "z"), fin)
    gathered = lax.all_gather(share, "seq")

    queries_out, key_rows, value_rows = [], [], []
    for i, (pairs, axes) in enumerate(PARTS):
        chunks = by_columns(second_kernel, sums[i], [208] * 4, "second")
        chunks = by_columns(third_kernel, exchange(chunks, axes[1]), [152] * 4, "third")
        query, key_part, value_part = by_columns(last_kernel, exchange(chunks, axes[2]), [128, 10, 10], "last")
        queries_out.append(jnp.stack(exchange([query] * 4, axes[0])))
        key_rows.append(key_part)
        value_rows.append(value_part)
    own_query = jnp.concatenate(queries_out, axis=2)
    other_query = shift(own_query, "c", 1)
    query_grad = pl.pallas_call(
        place_query_kernel,
        in_specs=[SMEM, vmem, vmem],
        out_shape=jax.ShapeDtypeStruct((L, D), F32),
        compiler_params=params(),
        cost_estimate=cost(1e6, 1e7),
        name="place_query",
    )(jnp.stack([core] + [own[axes[0]] for _, axes in PARTS]), own_query, other_query)

    attended = pl.pallas_call(
        round_kernel,
        grid=(16,),
        in_specs=[pl.BlockSpec((1, 128, 640), lambda i: (i, 0, 0))],
        out_specs=pl.BlockSpec((128, 640), lambda i: (i // 2, i % 2)),
        out_shape=jax.ShapeDtypeStruct((L, D), BF16),
        compiler_params=params(),
        cost_estimate=cost(1e6, 8e6),
        name="round",
    )(gathered)
    return (
        attended.reshape(1, L, D),
        query_grad,
        jnp.concatenate(key_rows, axis=1),
        jnp.concatenate(value_rows, axis=1),
    )


def solution(mesh):
    placed = (P("dp", "seq", None), P(), P(), P(), P("dp", None, None))
    return jax.shard_map(
        on_device,
        mesh=mesh,
        in_specs=placed,
        out_specs=(P("dp", None, None), P(), P(("seq", "dp"), None), P(("seq", "dp"), None)),
        check_vma=False,
    )
```

```python
import functools

import jax
import jax.numpy as jnp
import numpy as np
from jax import lax
from jax.experimental import pallas as pl
from jax.experimental.pallas import tpu as pltpu
from jax.sharding import PartitionSpec as P

H = 10
HD = 128
T = 512
L = 1024
D = 1280
PAIR = 2 * HD
SCALE = HD ** (-0.5)
VMEM_LIMIT = 56 * 1024 * 1024
PAIRS = H // 2
Z_GROUPS = [[a * 4 + b for b in range(4)] for a in range(4)]
Y_GROUPS = [[a * 2 + b for a in range(4)] for b in range(2)]
F32 = jnp.float32
BF16 = jnp.bfloat16


def shift(array, axis, step):
    if axis == "x":
        return lax.ppermute(array, "seq", [(a * 4 + b, (a + step) % 4 * 4 + b) for a in range(4) for b in range(4)])
    if axis == "z":
        return lax.ppermute(array, "seq", [(a * 4 + b, a * 4 + (b + step) % 4) for a in range(4) for b in range(4)])
    if axis == "y":
        return lax.ppermute(array, "dp", [(a * 2 + b, (a + step) % 4 * 2 + b) for a in range(4) for b in range(2)])
    return lax.ppermute(array, "dp", [(a * 2 + b, a * 2 + 1 - b) for a in range(4) for b in range(2)])


def nt_dot(a, b):
    return lax.dot_general(a, b, (((1,), (1,)), ((), ())), preferred_element_type=F32)


def dot(a, b):
    return jnp.dot(a, b, preferred_element_type=F32)


def params():
    return pltpu.CompilerParams(vmem_limit_bytes=VMEM_LIMIT)


def cost(flops, moved):
    return pl.CostEstimate(flops=int(flops), bytes_accessed=int(moved), transcendentals=0)


def full(shape):
    return pl.BlockSpec(shape, lambda *_: (0,) * len(shape))


SMEM = pl.BlockSpec(memory_space=pltpu.SMEM)


def forward_kernel(place, tok, kw, vw, q, g, k_out, v_out, normed_out, n0, n1, n2, n3, stats, normed, s, w, numer):
    @pl.when(pl.program_id(0) == 0)
    def _():
        values = tok[...].astype(F32)
        centre = values - jnp.mean(values, axis=-1, keepdims=True)
        spread = jnp.mean(centre * centre, axis=-1, keepdims=True)
        normed[...] = (centre * lax.rsqrt(spread + 1e-05)).astype(BF16)
        normed_out[...] = normed[...]

    keys = dot(normed[...], kw[...]).astype(BF16)
    vals = dot(normed[...], vw[...]).astype(BF16)
    k_out[...] = keys
    v_out[...] = vals
    vals_t = vals.T
    grad_t = g[...].T
    for j in range(2):
        head = slice(j * HD, (j + 1) * HD)
        s[j] = nt_dot(keys[:, head], q[:, head])
        tops, totals = [], []
        for tile in range(L // 128):
            at = slice(tile * 128, (tile + 1) * 128)
            scores = s[j, :, at] * SCALE
            high = jnp.max(scores, axis=0, keepdims=True)
            shifted = jnp.exp(scores - high)
            tops.append(high)
            totals.append(jnp.sum(shifted, axis=0, keepdims=True))
            w[j, :, at] = shifted.astype(BF16)
        total = jnp.concatenate(totals, axis=1)
        part = dot(vals_t[head, :], w[j]) * (1.0 / total)
        numer[head, :] = part
        stats[0, j : j + 1, :] = jnp.concatenate(tops, axis=1) + jnp.log(total)
        stats[0, 2 + j : 3 + j, :] = jnp.sum(part * grad_t[head, :].astype(F32), axis=0, keepdims=True)
    for k, out in enumerate((n0, n1, n2, n3)):
        start = pl.multiple_of(lax.rem(place[0] + k, 4) * 256, 256)
        out[...] = numer[:, pl.ds(start, 256)]


def forward(place, tokens, kw, vw, q, g):
    cols = lambda rows: pl.BlockSpec((rows, PAIR), lambda i: (0, i))
    return pl.pallas_call(
        forward_kernel,
        grid=(PAIRS,),
        in_specs=[SMEM, full((T, D)), cols(D), cols(D), cols(L), cols(L)],
        out_specs=[cols(T), cols(T), full((T, D))]
        + [pl.BlockSpec((PAIR, 256), lambda i: (i, 0))] * 4
        + [pl.BlockSpec((1, 4, L), lambda i: (i, 0, 0))],
        out_shape=[jax.ShapeDtypeStruct((T, D), BF16)] * 3
        + [jax.ShapeDtypeStruct((D, 256), F32)] * 4
        + [jax.ShapeDtypeStruct((PAIRS, 4, L), F32)],
        scratch_shapes=[
            pltpu.VMEM((T, D), BF16),
            pltpu.VMEM((2, T, L), F32),
            pltpu.VMEM((2, T, L), BF16),
            pltpu.VMEM((PAIR, L), F32),
        ],
        compiler_params=params(),
        cost_estimate=cost(1.2e10, 2.4e7),
        name="forward",
    )(place, tokens, kw, vw, q, g)


def merge_kernel(s0, s1, s2, s3, out):
    blocks = (s0, s1, s2, s3)
    top = functools.reduce(jnp.maximum, [b[:, 0:2, :] for b in blocks])
    total = jnp.zeros_like(top)
    inner = jnp.zeros_like(top)
    for b in blocks:
        factor = jnp.exp(b[:, 0:2, :] - top)
        total += factor
        inner += b[:, 2:4, :] * factor
    out[:, 0:2, :] = top + jnp.log(total)
    out[:, 2:4, :] = inner / total


def simple(kernel, ins, outs, name, scalars=None, scratch=(), moved=4e6, flops=1e6):
    specs = [pl.BlockSpec(memory_space=pltpu.VMEM)] * len(ins)
    several = isinstance(outs, list)
    shapes = [jax.ShapeDtypeStruct(o, F32) for o in (outs if several else [outs])]
    return pl.pallas_call(
        kernel,
        in_specs=([] if scalars is None else [SMEM]) + specs,
        out_shape=shapes if several else shapes[0],
        scratch_shapes=list(scratch),
        compiler_params=params(),
        cost_estimate=cost(flops, moved),
        name=name,
    )(*([] if scalars is None else [scalars]), *ins)


def reorder_kernel(order, normed, out):
    feature = lax.broadcasted_iota(jnp.int32, (D, D), 0)
    choose = jnp.where(feature == order[...], 1.0, 0.0).astype(BF16)
    out[...] = dot(normed[...], choose).astype(BF16).T


def reorder(order, normed):
    return pl.pallas_call(
        reorder_kernel,
        out_shape=jax.ShapeDtypeStruct((D, T), BF16),
        compiler_params=params(),
        cost_estimate=cost(2 * T * D * D, 3e6),
        name="reorder",
    )(order, normed)


def row_order(place):
    digits = [jnp.asarray(d, jnp.int32) for d in np.indices((2, 4, 4, 4, 10)).reshape(5, D)]
    core = (place[3] + digits[0]) % 2
    x = (place[0] + digits[2]) % 4
    z = (place[1] + digits[3]) % 4
    owner = ((x * 4 + z) * 4 + digits[1]) * 2 + core
    return (owner * 10 + digits[4]).reshape(1, D)


def pair_cols(rows):
    return pl.BlockSpec((rows, PAIR), lambda i: (0, i))


def value_kernel(nt, keys, q, g, fin, mine, theirs, s, p):
    grads = []
    for j in range(2):
        head = slice(j * HD, (j + 1) * HD)
        s[j] = nt_dot(keys[:, head], q[:, head])
        for tile in range(L // 128):
            at = slice(tile * 128, (tile + 1) * 128)
            p[j, :, at] = jnp.exp(s[j, :, at] * SCALE - fin[0, j : j + 1, at]).astype(BF16)
        grads.append(dot(p[j], g[:, head]).astype(BF16))
    rows = dot(nt[...], jnp.concatenate(grads, axis=1))
    mine[...] = rows[0:640]
    theirs[...] = rows[640:1280]


def key_kernel(place, nt, keys, vals, q, g, fin, mine, theirs, q_mine, q_theirs, s, pg, sg, query):
    grads = []
    keys_t = keys[...].T
    for j in range(2):
        head = slice(j * HD, (j + 1) * HD)
        s[j] = nt_dot(keys[:, head], q[:, head])
        pg[j] = nt_dot(vals[:, head], g[:, head])
        for tile in range(L // 128):
            at = slice(tile * 128, (tile + 1) * 128)
            probs = jnp.exp(s[j, :, at] * SCALE - fin[0, j : j + 1, at])
            sg[j, :, at] = (probs * (pg[j, :, at] - fin[0, 2 + j : 3 + j, at]) * SCALE).astype(BF16)
        query[:, head] = dot(keys_t[head, :], sg[j]).T
        grads.append(dot(sg[j], q[:, head]).astype(BF16))
    rows = dot(nt[...], jnp.concatenate(grads, axis=1))
    mine[...] = rows[0:640]
    theirs[...] = rows[640:1280]
    start = pl.multiple_of(place[3] * 512, 512)
    q_mine[...] = query[pl.ds(start, 512), :]
    q_theirs[...] = query[pl.ds(512 - start, 512), :]


def backward_specs():
    return [full((D, T)), pair_cols(T)], [pair_cols(L), pair_cols(L), pl.BlockSpec((1, 4, L), lambda i: (i, 0, 0))]


def value_grad(nt, keys, q, g, fin):
    first, rest = backward_specs()
    return pl.pallas_call(
        value_kernel,
        grid=(PAIRS,),
        in_specs=first + rest,
        out_specs=[pair_cols(640)] * 2,
        out_shape=[jax.ShapeDtypeStruct((640, D), F32)] * 2,
        scratch_shapes=[pltpu.VMEM((2, T, L), F32), pltpu.VMEM((2, T, L), BF16)],
        compiler_params=params(),
        cost_estimate=cost(8e9, 1.6e7),
        name="value_grad",
    )(nt, keys, q, g, fin)


def key_grad(place, nt, keys, vals, q, g, fin):
    first, rest = backward_specs()
    return pl.pallas_call(
        key_kernel,
        grid=(PAIRS,),
        in_specs=[SMEM] + first + [pair_cols(T)] + rest,
        out_specs=[pair_cols(640)] * 2 + [pair_cols(512)] * 2,
        out_shape=[jax.ShapeDtypeStruct((640, D), F32)] * 2 + [jax.ShapeDtypeStruct((512, D), F32)] * 2,
        scratch_shapes=[
            pltpu.VMEM((2, T, L), F32),
            pltpu.VMEM((2, T, L), F32),
            pltpu.VMEM((2, T, L), BF16),
            pltpu.VMEM((L, PAIR), F32),
        ],
        compiler_params=params(),
        cost_estimate=cost(1.6e10, 2.4e7),
        name="key_grad",
    )(place, nt, keys, vals, q, g, fin)


def four(a0, a1, a2, a3):
    return (a0[...] + a2[...]) + (a1[...] + a3[...])


def exchange(chunks, axis):
    far = {k: shift(chunks[k], axis, k) for k in (2, 1, 3)}
    return [chunks[0], far[1], far[2], far[3]]


def pair_kernel(place, mine, other, *outs):
    for k, out in enumerate(outs):
        start = pl.multiple_of(lax.rem(place[2] + k, 4) * 160, 160)
        out[...] = mine[pl.ds(start, 160), :] + other[pl.ds(start, 160), :]


def pair_chunks(place, mine, other):
    return pl.pallas_call(
        pair_kernel,
        grid=(PAIRS,),
        in_specs=[SMEM, pair_cols(640), pair_cols(640)],
        out_specs=[pair_cols(160)] * 4,
        out_shape=[jax.ShapeDtypeStruct((160, D), F32)] * 4,
        compiler_params=params(),
        cost_estimate=cost(1e6, 1e7),
        name="pair",
    )(place, mine, other)


def rows_x_kernel(value, a0, a1, a2, a3, *outs):
    rows = four(a0, a1, a2, a3)
    for k, out in enumerate(outs):
        out[0:40, :] = rows[k * 40 : (k + 1) * 40]
        out[40:80, :] = value[k * 40 : (k + 1) * 40, :]


def rows_z_kernel(a0, a1, a2, a3, *outs):
    rows = four(a0, a1, a2, a3)
    for k, out in enumerate(outs):
        out[0:10, :] = rows[k * 10 : (k + 1) * 10]
        out[10:20, :] = rows[40 + k * 10 : 40 + (k + 1) * 10]
        out[20:24, :] = jnp.zeros((4, D), F32)


def rows_last_kernel(a0, a1, a2, a3, key_rows, value_rows):
    rows = four(a0, a1, a2, a3)
    key_rows[...] = rows[0:10]
    value_rows[...] = rows[10:20]


def query_x_kernel(place, parts, *outs):
    rows = (parts[0] + parts[1]) + (parts[2] + parts[3])
    total = outs[-1]
    total[...] = rows
    for k, out in enumerate(outs[:-1]):
        start = pl.multiple_of(lax.rem(place[0] + k, 4) * 32, 32)
        out[...] = total[pl.ds(start, 32), :]


def query_sum_kernel(a0, a1, a2, a3, out):
    out[...] = four(a0, a1, a2, a3)


def query_halves_kernel(a0, a1, a2, a3, left, right):
    rows = four(a0, a1, a2, a3)
    left[...] = rows[:, 0:640]
    right[...] = rows[:, 640:1280]


def place_query_kernel(place, own, other, out):
    for half, block in ((place[3], own), (1 - place[3], other)):
        for i in range(4):
            for k in range(4):
                first = lax.rem(place[1] + 4 - i, 4) * 128 + lax.rem(place[0] + 4 - k, 4) * 32
                out[pl.ds(pl.multiple_of(half * 512 + first, 32), 32), 0:640] = block[i, k, :, 0:640]
                first = lax.rem(place[1] + 4 - k, 4) * 128 + lax.rem(place[0] + 4 - i, 4) * 32
                out[pl.ds(pl.multiple_of(half * 512 + first, 32), 32), 640:1280] = block[i, k, :, 640:1280]


def numer_x_kernel(place, n0, n1, n2, n3, s0, s1, s2, s3, fin, z0, z1, z2, z3, total):
    at = pl.ds(pl.multiple_of(place[0] * 256, 256), 256)
    for h in range(H):
        rows = slice(h * HD, (h + 1) * HD)
        pair, j = h // 2, h % 2
        acc = jnp.zeros((HD, 256), F32)
        for n, s in ((n0, s0), (n1, s1), (n2, s2), (n3, s3)):
            acc += n[rows, :] * jnp.exp(s[pair, j : j + 1, at] - fin[pair, j : j + 1, at])
        total[rows, :] = acc
    for k, out in enumerate((z0, z1, z2, z3)):
        spot = lax.rem(place[1] + k, 4)
        row = pl.multiple_of(lax.rem(spot, 2) * 640, 640)
        lane = pl.multiple_of(lax.div(spot, 2) * 128, 128)
        out[...] = total[pl.ds(row, 640), pl.ds(lane, 128)]


def numer_z_kernel(z0, z1, z2, z3, out):
    out[...] = four(z0, z1, z2, z3).T


def round_kernel(x, out):
    for k in range(2):
        rows = slice(k * 128, (k + 1) * 128)
        out[rows, 0:640] = x[2 * k].astype(BF16)
        out[rows, 640:1280] = x[2 * k + 1].astype(BF16)


def on_device(tokens, queries, key_weight, value_weight, out_grad):
    seq, dp = lax.axis_index("seq"), lax.axis_index("dp")
    place = jnp.stack([seq // 4, seq % 4, dp // 2, dp % 2]).astype(jnp.int32)
    grad = out_grad[0]

    keys, vals, normed, n0, n1, n2, n3, stats = forward(place, tokens[0], key_weight, value_weight, queries, grad)
    near = exchange([stats] * 4, "x")
    nt = reorder(row_order(place), normed)
    near, nt, n1, n2, n3 = lax.optimization_barrier((near, nt, n1, n2, n3))
    group = simple(merge_kernel, near, (PAIRS, 4, L), "merge")
    blocks = exchange([group] * 4, "z")
    numer = exchange([n0, n1, n2, n3], "x")
    fin = simple(merge_kernel, blocks, (PAIRS, 4, L), "finish")

    v_mine, v_theirs = value_grad(nt, keys, queries, grad, fin)
    v_other = shift(v_theirs, "c", 1)
    k_mine, k_theirs, q_mine, q_theirs = key_grad(place, nt, keys, vals, queries, grad, fin)
    q_other = shift(q_theirs, "c", 1)
    k_other = shift(k_theirs, "c", 1)

    v_rows = lax.psum_scatter(
        (v_mine + v_other).reshape(4, 160, D), "dp", scatter_dimension=0, axis_index_groups=Y_GROUPS, tiled=False
    )
    k_chunks = exchange(pair_chunks(place, k_mine, k_other), "y")

    q_parts = lax.all_to_all(
        (q_mine + q_other).reshape(4, 128, D), "seq", split_axis=0, concat_axis=0, axis_index_groups=Z_GROUPS
    )
    q_parts = simple(
        query_x_kernel, [q_parts], [(32, D)] * 4, "query_x", scalars=place, scratch=[pltpu.VMEM((128, D), F32)]
    )
    q_part = simple(query_sum_kernel, exchange(q_parts, "x"), (32, D), "query_sum")
    left, right = simple(query_halves_kernel, exchange([q_part] * 4, "y"), [(32, 640)] * 2, "query_halves")
    left = jnp.stack(exchange([left] * 4, "x"))
    right = jnp.stack(exchange([right] * 4, "z"))
    left = jnp.stack(exchange([left] * 4, "z"))
    right = jnp.stack(exchange([right] * 4, "x"))
    own_query = jnp.concatenate([left, right], axis=3)

    zs = simple(
        numer_x_kernel,
        [*numer, *near, fin],
        [(640, 128)] * 4,
        "numer_x",
        scalars=place,
        scratch=[pltpu.VMEM((D, 256), F32)],
        moved=7e6,
    )
    share = simple(numer_z_kernel, exchange(zs, "z"), (128, 640), "numer_z")
    gathered = lax.all_gather(share, "seq")
    attended = pl.pallas_call(
        round_kernel,
        grid=(4,),
        in_specs=[pl.BlockSpec((4, 128, 640), lambda i: (i, 0, 0))],
        out_specs=pl.BlockSpec((256, D), lambda i: (i, 0)),
        out_shape=jax.ShapeDtypeStruct((L, D), BF16),
        compiler_params=params(),
        cost_estimate=cost(1e6, 8e6),
        name="round",
    )(gathered)

    rows = simple(rows_x_kernel, [v_rows, *k_chunks], [(80, D)] * 4, "rows_x")
    rows = simple(rows_z_kernel, exchange(rows, "x"), [(24, D)] * 4, "rows_z")
    key_rows, value_rows = simple(rows_last_kernel, exchange(rows, "z"), [(10, D)] * 2, "rows_last")

    own_query, attended, key_rows, value_rows = lax.optimization_barrier((own_query, attended, key_rows, value_rows))
    other_query = shift(own_query, "c", 1)
    query_grad = simple(place_query_kernel, [own_query, other_query], (L, D), "place_query", scalars=place, moved=1e7)
    return attended.reshape(1, L, D), query_grad, key_rows, value_rows


def solution(mesh):
    placed = (P("dp", "seq", None), P(), P(), P(), P("dp", None, None))
    return jax.shard_map(
        on_device,
        mesh=mesh,
        in_specs=placed,
        out_specs=(P("dp", None, None), P(), P(("seq", "dp"), None), P(("seq", "dp"), None)),
        check_vma=False,
    )
```

```python
import functools

import jax
import jax.numpy as jnp
import numpy as np
from jax import lax
from jax.experimental import pallas as pl
from jax.experimental.pallas import tpu as pltpu
from jax.sharding import PartitionSpec as P

H = 10
HD = 128
T = 512
L = 1024
D = 1280
PAIR = 2 * HD
SCALE = HD ** (-0.5)
VMEM_LIMIT = 56 * 1024 * 1024
PAIRS = H // 2
COST = 1.0
PAIR_GROUPS = [[a * 2, a * 2 + 1] for a in range(4)]
CORE_GROUPS = [[a * 2 + b for a in range(64)] for b in range(2)]
F32 = jnp.float32
BF16 = jnp.bfloat16


def shift(array, axis, step):
    if axis == "x":
        return lax.ppermute(array, "seq", [(a * 4 + b, (a + step) % 4 * 4 + b) for a in range(4) for b in range(4)])
    if axis == "z":
        return lax.ppermute(array, "seq", [(a * 4 + b, a * 4 + (b + step) % 4) for a in range(4) for b in range(4)])
    if axis == "y":
        return lax.ppermute(array, "dp", [(a * 2 + b, (a + step) % 4 * 2 + b) for a in range(4) for b in range(2)])
    return lax.ppermute(array, "dp", [(a * 2 + b, a * 2 + 1 - b) for a in range(4) for b in range(2)])


def nt_dot(a, b):
    return lax.dot_general(a, b, (((1,), (1,)), ((), ())), preferred_element_type=F32)


def dot(a, b):
    return jnp.dot(a, b, preferred_element_type=F32)


def params():
    return pltpu.CompilerParams(vmem_limit_bytes=VMEM_LIMIT)


def cost(flops, moved):
    return pl.CostEstimate(flops=int(flops * COST), bytes_accessed=int(moved * COST), transcendentals=0)


def full(shape):
    return pl.BlockSpec(shape, lambda *_: (0,) * len(shape))


SMEM = pl.BlockSpec(memory_space=pltpu.SMEM)


def forward_kernel(place, tok, kw, vw, q, g, k_out, v_out, normed_out, n0, n1, n2, n3, stats, normed, s, w, numer):
    @pl.when(pl.program_id(0) == 0)
    def _():
        values = tok[...].astype(F32)
        centre = values - jnp.mean(values, axis=-1, keepdims=True)
        spread = jnp.mean(centre * centre, axis=-1, keepdims=True)
        normed[...] = (centre * lax.rsqrt(spread + 1e-05)).astype(BF16)
        normed_out[...] = normed[...]

    keys = dot(normed[...], kw[...]).astype(BF16)
    vals = dot(normed[...], vw[...]).astype(BF16)
    k_out[...] = keys
    v_out[...] = vals
    vals_t = vals.T
    grad_t = g[...].T
    for j in range(2):
        head = slice(j * HD, (j + 1) * HD)
        s[j] = nt_dot(keys[:, head], q[:, head])
        tops, totals = [], []
        for tile in range(L // 128):
            at = slice(tile * 128, (tile + 1) * 128)
            scores = s[j, :, at] * SCALE
            high = jnp.max(scores, axis=0, keepdims=True)
            shifted = jnp.exp(scores - high)
            tops.append(high)
            totals.append(jnp.sum(shifted, axis=0, keepdims=True))
            w[j, :, at] = shifted.astype(BF16)
        total = jnp.concatenate(totals, axis=1)
        part = dot(vals_t[head, :], w[j]) * (1.0 / total)
        numer[head, :] = part
        stats[0, j : j + 1, :] = jnp.concatenate(tops, axis=1) + jnp.log(total)
        stats[0, 2 + j : 3 + j, :] = jnp.sum(part * grad_t[head, :].astype(F32), axis=0, keepdims=True)
    for k, out in enumerate((n0, n1, n2, n3)):
        start = pl.multiple_of(lax.rem(place[0] + k, 4) * 256, 256)
        out[...] = numer[:, pl.ds(start, 256)]


def forward(place, tokens, kw, vw, q, g):
    cols = lambda rows: pl.BlockSpec((rows, PAIR), lambda i: (0, i))
    return pl.pallas_call(
        forward_kernel,
        grid=(PAIRS,),
        in_specs=[SMEM, full((T, D)), cols(D), cols(D), cols(L), cols(L)],
        out_specs=[cols(T), cols(T), full((T, D))]
        + [pl.BlockSpec((PAIR, 256), lambda i: (i, 0))] * 4
        + [pl.BlockSpec((1, 4, L), lambda i: (i, 0, 0))],
        out_shape=[jax.ShapeDtypeStruct((T, D), BF16)] * 3
        + [jax.ShapeDtypeStruct((D, 256), F32)] * 4
        + [jax.ShapeDtypeStruct((PAIRS, 4, L), F32)],
        scratch_shapes=[
            pltpu.VMEM((T, D), BF16),
            pltpu.VMEM((2, T, L), F32),
            pltpu.VMEM((2, T, L), BF16),
            pltpu.VMEM((PAIR, L), F32),
        ],
        compiler_params=params(),
        cost_estimate=cost(1.2e10, 2.4e7),
        name="forward",
    )(place, tokens, kw, vw, q, g)


def merge_kernel(s0, s1, s2, s3, out):
    blocks = (s0, s1, s2, s3)
    top = functools.reduce(jnp.maximum, [b[:, 0:2, :] for b in blocks])
    total = jnp.zeros_like(top)
    inner = jnp.zeros_like(top)
    for b in blocks:
        factor = jnp.exp(b[:, 0:2, :] - top)
        total += factor
        inner += b[:, 2:4, :] * factor
    out[:, 0:2, :] = top + jnp.log(total)
    out[:, 2:4, :] = inner / total


def simple(kernel, ins, outs, name, scalars=None, scratch=(), moved=4e6, flops=1e6):
    specs = [pl.BlockSpec(memory_space=pltpu.VMEM)] * len(ins)
    several = isinstance(outs, list)
    shapes = [jax.ShapeDtypeStruct(o, F32) for o in (outs if several else [outs])]
    return pl.pallas_call(
        kernel,
        in_specs=([] if scalars is None else [SMEM]) + specs,
        out_shape=shapes if several else shapes[0],
        scratch_shapes=list(scratch),
        compiler_params=params(),
        cost_estimate=cost(flops, moved),
        name=name,
    )(*([] if scalars is None else [scalars]), *ins)


def reorder_kernel(order, normed, out):
    feature = lax.broadcasted_iota(jnp.int32, (D, D), 0)
    choose = jnp.where(feature == order[...], 1.0, 0.0).astype(BF16)
    out[...] = dot(normed[...], choose).astype(BF16).T


def reorder(order, normed):
    return pl.pallas_call(
        reorder_kernel,
        out_shape=jax.ShapeDtypeStruct((D, T), BF16),
        compiler_params=params(),
        cost_estimate=cost(2 * T * D * D, 3e6),
        name="reorder",
    )(order, normed)


def row_order(place):
    digits = [jnp.asarray(d, jnp.int32) for d in np.indices((4, 2, 4, 4, 10)).reshape(5, D)]
    z = (place[1] + digits[2]) % 4
    x = (place[0] + digits[3]) % 4
    owner = ((x * 4 + z) * 4 + digits[0]) * 2 + digits[1]
    return (owner * 10 + digits[4]).reshape(1, D)


def pair_cols(rows):
    return pl.BlockSpec((rows, PAIR), lambda i: (0, i))


def backward_kernel(nt, keys, vals, q, g, fin, out, q_out, s, pg, p, sg, kgrad, vgrad):
    keys_t = keys[...].T
    for j in range(2):
        head = slice(j * HD, (j + 1) * HD)
        s[j] = nt_dot(keys[:, head], q[:, head])
        pg[j] = nt_dot(vals[:, head], g[:, head])
        for tile in range(L // 128):
            at = slice(tile * 128, (tile + 1) * 128)
            probs = jnp.exp(s[j, :, at] * SCALE - fin[0, j : j + 1, at])
            p[j, :, at] = probs.astype(BF16)
            sg[j, :, at] = (probs * (pg[j, :, at] - fin[0, 2 + j : 3 + j, at]) * SCALE).astype(BF16)
        query = dot(keys_t[head, :], sg[j]).T
        for half in range(2):
            for block in range(64):
                row = half * 512 + block % 4 * 128 + block // 4 * 8
                q_out[half, block, :, head] = query[row : row + 8, :]
        kgrad[:, head] = dot(sg[j], q[:, head]).astype(BF16)
        vgrad[:, head] = dot(p[j], g[:, head]).astype(BF16)
    out[:, 0:PAIR] = dot(nt[...], kgrad[...])
    out[:, PAIR:] = dot(nt[...], vgrad[...])


def backward(nt, keys, vals, q, g, fin):
    return pl.pallas_call(
        backward_kernel,
        grid=(PAIRS,),
        in_specs=[
            full((D, T)),
            pair_cols(T),
            pair_cols(T),
            pair_cols(L),
            pair_cols(L),
            pl.BlockSpec((1, 4, L), lambda i: (i, 0, 0)),
        ],
        out_specs=[
            pl.BlockSpec((D, 2 * PAIR), lambda i: (0, i)),
            pl.BlockSpec((2, 64, 8, PAIR), lambda i: (0, 0, 0, i)),
        ],
        out_shape=[jax.ShapeDtypeStruct((D, 2 * D), F32), jax.ShapeDtypeStruct((2, 64, 8, D), F32)],
        scratch_shapes=[
            pltpu.VMEM((2, T, L), F32),
            pltpu.VMEM((2, T, L), F32),
            pltpu.VMEM((2, T, L), BF16),
            pltpu.VMEM((2, T, L), BF16),
            pltpu.VMEM((T, PAIR), BF16),
            pltpu.VMEM((T, PAIR), BF16),
        ],
        compiler_params=params(),
        cost_estimate=cost(2e10, 3.0e7),
        name="backward",
    )(nt, keys, vals, q, g, fin)


def four(a0, a1, a2, a3):
    return (a0[...] + a2[...]) + (a1[...] + a3[...])


def exchange(chunks, axis):
    far = {k: shift(chunks[k], axis, k) for k in (2, 1, 3)}
    return [chunks[0], far[1], far[2], far[3]]


def second_kernel(rows, *outs):
    for k, out in enumerate(outs):
        out[...] = rows[k * 40 : (k + 1) * 40]


def third_kernel(a0, a1, a2, a3, *outs):
    rows = four(a0, a1, a2, a3)
    for k, out in enumerate(outs):
        out[0:10, :] = rows[k * 10 : (k + 1) * 10]
        out[10:16, :] = jnp.zeros((6, 2 * D), F32)


def last_kernel(a0, a1, a2, a3, key_rows, value_rows):
    rows = four(a0, a1, a2, a3)
    for i in range(PAIRS):
        cols = slice(i * PAIR, (i + 1) * PAIR)
        key_rows[:, cols] = rows[0:10, 2 * i * PAIR : (2 * i + 1) * PAIR]
        value_rows[:, cols] = rows[0:10, (2 * i + 1) * PAIR : (2 * i + 2) * PAIR]


def query_sum_kernel(parts, out):
    rows = parts[0]
    for k in range(1, 64):
        rows += parts[k]
    for k in range(16):
        out[k] = rows


def query_sum(parts):
    return pl.pallas_call(
        query_sum_kernel,
        grid=(PAIRS,),
        in_specs=[pl.BlockSpec((64, 8, PAIR), lambda i: (0, 0, i))],
        out_specs=pl.BlockSpec((16, 8, PAIR), lambda i: (0, 0, i)),
        out_shape=jax.ShapeDtypeStruct((16, 8, D), F32),
        compiler_params=params(),
        cost_estimate=cost(1e6, 4e6),
        name="query_sum",
    )(parts)


def place_query_kernel(place, own, other, out):
    for k in range(4):
        block = lax.rem(place[2] + 4 - k, 4) * 128
        out[pl.ds(pl.multiple_of(place[3] * 512 + block, 128), 128), :] = own[k]
        out[pl.ds(pl.multiple_of((1 - place[3]) * 512 + block, 128), 128), :] = other[k]


def place_query(place, own, other):
    return pl.pallas_call(
        place_query_kernel,
        grid=(PAIRS,),
        in_specs=[SMEM] + [pl.BlockSpec((4, 128, PAIR), lambda i: (0, 0, i))] * 2,
        out_specs=pair_cols(L),
        out_shape=jax.ShapeDtypeStruct((L, D), F32),
        compiler_params=params(),
        cost_estimate=cost(1e6, 1e7),
        name="place_query",
    )(place, own, other)


def spread(blocks):
    return lax.all_to_all(blocks, ("seq", "dp"), split_axis=0, concat_axis=0, axis_index_groups=CORE_GROUPS)


def numer_x_kernel(place, n0, n1, n2, n3, s0, s1, s2, s3, fin, z0, z1, z2, z3, total):
    at = pl.ds(pl.multiple_of(place[0] * 256, 256), 256)
    for h in range(H):
        rows = slice(h * HD, (h + 1) * HD)
        pair, j = h // 2, h % 2
        acc = jnp.zeros((HD, 256), F32)
        for n, s in ((n0, s0), (n1, s1), (n2, s2), (n3, s3)):
            acc += n[rows, :] * jnp.exp(s[pair, j : j + 1, at] - fin[pair, j : j + 1, at])
        total[rows, :] = acc
    for k, out in enumerate((z0, z1, z2, z3)):
        spot = lax.rem(place[1] + k, 4)
        row = pl.multiple_of(lax.rem(spot, 2) * 640, 640)
        lane = pl.multiple_of(lax.div(spot, 2) * 128, 128)
        out[...] = total[pl.ds(row, 640), pl.ds(lane, 128)]


def numer_z_kernel(z0, z1, z2, z3, out):
    out[...] = four(z0, z1, z2, z3).T


def round_kernel(x, out):
    for k in range(2):
        rows = slice(k * 128, (k + 1) * 128)
        out[rows, 0:640] = x[2 * k].astype(BF16)
        out[rows, 640:1280] = x[2 * k + 1].astype(BF16)


def after(first, values):
    return lax.optimization_barrier((first, values))[1]


def on_device(tokens, queries, key_weight, value_weight, out_grad):
    seq, dp = lax.axis_index("seq"), lax.axis_index("dp")
    place = jnp.stack([seq // 4, seq % 4, dp // 2, dp % 2]).astype(jnp.int32)
    grad = out_grad[0]

    keys, vals, normed, n0, n1, n2, n3, stats = forward(place, tokens[0], key_weight, value_weight, queries, grad)
    near = exchange([stats] * 4, "x")
    nt = reorder(row_order(place), normed)
    near, nt, n1, n2, n3 = lax.optimization_barrier((near, nt, n1, n2, n3))
    group = simple(merge_kernel, near, (PAIRS, 4, L), "merge")
    blocks = exchange([group] * 4, "z")
    numer = exchange([n0, n1, n2, n3], "x")
    fin = simple(merge_kernel, blocks, (PAIRS, 4, L), "finish")

    terms, q_terms = backward(nt, keys, vals, queries, grad, fin)
    q_cores = lax.all_to_all(q_terms, "dp", split_axis=0, concat_axis=0, axis_index_groups=PAIR_GROUPS)
    q_sum = q_cores[0] + q_cores[1]
    q_parts = spread(q_sum)
    numer, near = after(q_sum, (numer, near))
    rows = lax.psum_scatter(after(numer, terms), "dp", scatter_dimension=0, tiled=True)
    own_query = lax.all_to_all(query_sum(q_parts), "seq", split_axis=0, concat_axis=0).reshape(128, D)

    zs = simple(
        numer_x_kernel,
        [*numer, *near, fin],
        [(640, 128)] * 4,
        "numer_x",
        scalars=place,
        scratch=[pltpu.VMEM((D, 256), F32)],
        moved=7e6,
    )
    share = simple(numer_z_kernel, exchange(zs, "z"), (128, 640), "numer_z")
    gathered = lax.all_gather(after(q_parts, share), "seq")
    rows = after(own_query, rows)
    own_query = jnp.stack(exchange([own_query] * 4, "y"))

    attended = pl.pallas_call(
        round_kernel,
        grid=(4,),
        in_specs=[pl.BlockSpec((4, 128, 640), lambda i: (i, 0, 0))],
        out_specs=pl.BlockSpec((256, D), lambda i: (i, 0)),
        out_shape=jax.ShapeDtypeStruct((L, D), BF16),
        compiler_params=params(),
        cost_estimate=cost(1e6, 8e6),
        name="round",
    )(gathered)
    other_query = shift(own_query, "c", 1)
    query_grad = place_query(place, own_query, other_query)
    rows = exchange(simple(second_kernel, [rows], [(40, 2 * D)] * 4, "second"), "z")
    rows = exchange(simple(third_kernel, after(attended, rows), [(16, 2 * D)] * 4, "third"), "x")
    key_rows, value_rows = simple(last_kernel, after(query_grad, rows), [(10, D)] * 2, "last")
    return attended.reshape(1, L, D), query_grad, key_rows, value_rows


def solution(mesh):
    placed = (P("dp", "seq", None), P(), P(), P(), P("dp", None, None))
    return jax.shard_map(
        on_device,
        mesh=mesh,
        in_specs=placed,
        out_specs=(P("dp", None, None), P(), P(("seq", "dp"), None), P(("seq", "dp"), None)),
        check_vma=False,
    )
```

```python
import functools

import jax
import jax.numpy as jnp
import numpy as np
from jax import lax
from jax.experimental import pallas as pl
from jax.experimental.pallas import tpu as pltpu
from jax.sharding import PartitionSpec as P

H = 10
HD = 128
T = 512
L = 1024
D = 1280
PAIR = 2 * HD
SCALE = HD ** (-0.5)
SCALE2 = SCALE * 1.4426950408889634
VMEM_LIMIT = 56 * 1024 * 1024
PAIRS = H // 2
COST = 1.0
PAIR_GROUPS = [[a * 2, a * 2 + 1] for a in range(4)]
PLANE_GROUPS = [[a * 32 + b * 2 + c for b in range(16)] for a in range(4) for c in range(2)]
CORE_GROUPS = [[a * 2 + b for a in range(64)] for b in range(2)]
F32 = jnp.float32
BF16 = jnp.bfloat16


def shift(array, axis, step):
    if axis == "x":
        return lax.ppermute(array, "seq", [(a * 4 + b, (a + step) % 4 * 4 + b) for a in range(4) for b in range(4)])
    if axis == "z":
        return lax.ppermute(array, "seq", [(a * 4 + b, a * 4 + (b + step) % 4) for a in range(4) for b in range(4)])
    if axis == "y":
        return lax.ppermute(array, "dp", [(a * 2 + b, (a + step) % 4 * 2 + b) for a in range(4) for b in range(2)])
    return lax.ppermute(array, "dp", [(a * 2 + b, a * 2 + 1 - b) for a in range(4) for b in range(2)])


def nt_dot(a, b):
    return lax.dot_general(a, b, (((1,), (1,)), ((), ())), preferred_element_type=F32)


def dot(a, b):
    return jnp.dot(a, b, preferred_element_type=F32)


def params():
    return pltpu.CompilerParams(vmem_limit_bytes=VMEM_LIMIT)


def cost(flops, moved):
    return pl.CostEstimate(flops=int(flops * COST), bytes_accessed=int(moved * COST), transcendentals=0)


def full(shape):
    return pl.BlockSpec(shape, lambda *_: (0,) * len(shape))


SMEM = pl.BlockSpec(memory_space=pltpu.SMEM)


def forward_kernel(place, tok, kw, vw, q, g, k_out, v_out, normed_out, n0, n1, n2, n3, stats, normed, s, w, numer):
    @pl.when(pl.program_id(0) == 0)
    def _():
        values = tok[...].astype(F32)
        centre = values - jnp.mean(values, axis=-1, keepdims=True)
        spread = jnp.mean(centre * centre, axis=-1, keepdims=True)
        normed[...] = (centre * lax.rsqrt(spread + 1e-05)).astype(BF16)
        normed_out[...] = normed[...]

    keys = dot(normed[...], kw[...]).astype(BF16)
    vals = dot(normed[...], vw[...]).astype(BF16)
    k_out[...] = keys
    v_out[...] = vals
    vals_t = vals.T
    grad_t = g[...].T
    for j in range(2):
        head = slice(j * HD, (j + 1) * HD)
        tops, totals = [], []
        for tile in range(L // 256):
            at = slice(tile * 256, (tile + 1) * 256)
            scores = nt_dot(keys[:, head], q[at, head])
            high = jnp.max(scores, axis=0, keepdims=True) * SCALE2
            shifted = jnp.exp2(scores * SCALE2 - high)
            tops.append(high)
            totals.append(jnp.sum(shifted, axis=0, keepdims=True))
            w[j, :, at] = shifted.astype(BF16)
        total = jnp.concatenate(totals, axis=1)
        part = dot(vals_t[head, :], w[j]) * (1.0 / total)
        numer[head, :] = part
        stats[0, j : j + 1, :] = jnp.concatenate(tops, axis=1) + jnp.log2(total)
        stats[0, 2 + j : 3 + j, :] = jnp.sum(part * grad_t[head, :].astype(F32), axis=0, keepdims=True)
    for k, out in enumerate((n0, n1, n2, n3)):
        start = pl.multiple_of(lax.rem(place[0] + k, 4) * 256, 256)
        out[...] = numer[:, pl.ds(start, 256)]


def forward(place, tokens, kw, vw, q, g):
    cols = lambda rows: pl.BlockSpec((rows, PAIR), lambda i: (0, i))
    return pl.pallas_call(
        forward_kernel,
        grid=(PAIRS,),
        in_specs=[SMEM, full((T, D)), cols(D), cols(D), cols(L), cols(L)],
        out_specs=[cols(T), cols(T), full((T, D))]
        + [pl.BlockSpec((PAIR, 256), lambda i: (i, 0))] * 4
        + [pl.BlockSpec((1, 4, L), lambda i: (i, 0, 0))],
        out_shape=[jax.ShapeDtypeStruct((T, D), BF16)] * 3
        + [jax.ShapeDtypeStruct((D, 256), F32)] * 4
        + [jax.ShapeDtypeStruct((PAIRS, 4, L), F32)],
        scratch_shapes=[
            pltpu.VMEM((T, D), BF16),
            pltpu.VMEM((2, T, L), F32),
            pltpu.VMEM((2, T, L), BF16),
            pltpu.VMEM((PAIR, L), F32),
        ],
        compiler_params=params(),
        cost_estimate=cost(1.2e10, 2.4e7),
        name="forward",
    )(place, tokens, kw, vw, q, g)


def merge_kernel(s0, s1, s2, s3, out):
    blocks = (s0, s1, s2, s3)
    top = functools.reduce(jnp.maximum, [b[:, 0:2, :] for b in blocks])
    total = jnp.zeros_like(top)
    inner = jnp.zeros_like(top)
    for b in blocks:
        factor = jnp.exp2(b[:, 0:2, :] - top)
        total += factor
        inner += b[:, 2:4, :] * factor
    out[:, 0:2, :] = top + jnp.log2(total)
    out[:, 2:4, :] = inner / total


def simple(kernel, ins, outs, name, scalars=None, scratch=(), moved=4e6, flops=1e6):
    specs = [pl.BlockSpec(memory_space=pltpu.VMEM)] * len(ins)
    several = isinstance(outs, list)
    shapes = [jax.ShapeDtypeStruct(o, F32) for o in (outs if several else [outs])]
    return pl.pallas_call(
        kernel,
        in_specs=([] if scalars is None else [SMEM]) + specs,
        out_shape=shapes if several else shapes[0],
        scratch_shapes=list(scratch),
        compiler_params=params(),
        cost_estimate=cost(flops, moved),
        name=name,
    )(*([] if scalars is None else [scalars]), *ins)


def reorder_kernel(order, normed, out):
    feature = lax.broadcasted_iota(jnp.int32, (D, D), 0)
    choose = jnp.where(feature == order[...], 1.0, 0.0).astype(BF16)
    out[...] = dot(normed[...], choose).astype(BF16).T


def reorder(order, normed):
    return pl.pallas_call(
        reorder_kernel,
        out_shape=jax.ShapeDtypeStruct((D, T), BF16),
        compiler_params=params(),
        cost_estimate=cost(2 * T * D * D, 3e6),
        name="reorder",
    )(order, normed)


def row_order(place):
    digits = [jnp.asarray(d, jnp.int32) for d in np.indices((4, 2, 4, 4, 10)).reshape(5, D)]
    z = (place[1] + digits[2]) % 4
    x = (place[0] + digits[3]) % 4
    owner = ((x * 4 + z) * 4 + digits[0]) * 2 + digits[1]
    return (owner * 10 + digits[4]).reshape(1, D)


def pair_cols(rows):
    return pl.BlockSpec((rows, PAIR), lambda i: (0, i))


def backward_kernel(nt, keys, vals, q, g, fin, out, q_out, s, pg, p, sg, kgrad, vgrad):
    keys_t = keys[...].T
    for j in range(2):
        head = slice(j * HD, (j + 1) * HD)
        for tile in range(L // 256):
            at = slice(tile * 256, (tile + 1) * 256)
            probs = jnp.exp2(nt_dot(keys[:, head], q[at, head]) * SCALE2 - fin[0, j : j + 1, at])
            p[j, :, at] = probs.astype(BF16)
            sg[j, :, at] = (probs * (nt_dot(vals[:, head], g[at, head]) - fin[0, 2 + j : 3 + j, at]) * SCALE).astype(BF16)
        query = dot(keys_t[head, :], sg[j]).T
        q_out[:, :, :, head] = query.reshape(2, 64, 8, HD)
        kgrad[:, head] = dot(sg[j], q[:, head]).astype(BF16)
        vgrad[:, head] = dot(p[j], g[:, head]).astype(BF16)
    out[:, 0:PAIR] = dot(nt[...], kgrad[...])
    out[:, PAIR:] = dot(nt[...], vgrad[...])


def backward(nt, keys, vals, q, g, fin):
    return pl.pallas_call(
        backward_kernel,
        grid=(PAIRS,),
        in_specs=[
            full((D, T)),
            pair_cols(T),
            pair_cols(T),
            pair_cols(L),
            pair_cols(L),
            pl.BlockSpec((1, 4, L), lambda i: (i, 0, 0)),
        ],
        out_specs=[
            pl.BlockSpec((D, 2 * PAIR), lambda i: (0, i)),
            pl.BlockSpec((2, 64, 8, PAIR), lambda i: (0, 0, 0, i)),
        ],
        out_shape=[jax.ShapeDtypeStruct((D, 2 * D), F32), jax.ShapeDtypeStruct((2, 64, 8, D), F32)],
        scratch_shapes=[
            pltpu.VMEM((2, T, L), F32),
            pltpu.VMEM((2, T, L), F32),
            pltpu.VMEM((2, T, L), BF16),
            pltpu.VMEM((2, T, L), BF16),
            pltpu.VMEM((T, PAIR), BF16),
            pltpu.VMEM((T, PAIR), BF16),
        ],
        compiler_params=params(),
        cost_estimate=cost(2e10, 3.0e7),
        name="backward",
    )(nt, keys, vals, q, g, fin)


def four(a0, a1, a2, a3):
    return (a0[...] + a2[...]) + (a1[...] + a3[...])


def exchange(chunks, axis):
    far = {k: shift(chunks[k], axis, k) for k in (2, 1, 3)}
    return [chunks[0], far[1], far[2], far[3]]


def second_kernel(rows, *outs):
    for k, out in enumerate(outs):
        out[...] = rows[k * 40 : (k + 1) * 40]


def third_kernel(a0, a1, a2, a3, *outs):
    rows = four(a0, a1, a2, a3)
    for k, out in enumerate(outs):
        out[0:10, :] = rows[k * 10 : (k + 1) * 10]
        out[10:16, :] = jnp.zeros((6, 2 * D), F32)


def last_kernel(a0, a1, a2, a3, key_rows, value_rows):
    rows = four(a0, a1, a2, a3)
    for i in range(PAIRS):
        cols = slice(i * PAIR, (i + 1) * PAIR)
        key_rows[:, cols] = rows[0:10, 2 * i * PAIR : (2 * i + 1) * PAIR]
        value_rows[:, cols] = rows[0:10, (2 * i + 1) * PAIR : (2 * i + 2) * PAIR]


def query_sum_kernel(parts, out):
    rows = parts[0]
    for k in range(1, 64):
        rows += parts[k]
    for k in range(16):
        out[k] = rows


def query_sum(parts):
    return pl.pallas_call(
        query_sum_kernel,
        grid=(PAIRS,),
        in_specs=[pl.BlockSpec((64, 8, PAIR), lambda i: (0, 0, i))],
        out_specs=pl.BlockSpec((16, 8, PAIR), lambda i: (0, 0, i)),
        out_shape=jax.ShapeDtypeStruct((16, 8, D), F32),
        compiler_params=params(),
        cost_estimate=cost(1e6, 4e6),
        name="query_sum",
    )(parts)


def place_query_kernel(place, own, other, out):
    for k in range(4):
        block = lax.rem(place[0] + 4 - k, 4) * 128
        out[pl.ds(pl.multiple_of(place[3] * 512 + block, 128), 128), :] = own[k]
        out[pl.ds(pl.multiple_of((1 - place[3]) * 512 + block, 128), 128), :] = other[k]


def place_query(place, own, other):
    return pl.pallas_call(
        place_query_kernel,
        grid=(PAIRS,),
        in_specs=[SMEM] + [pl.BlockSpec((4, 128, PAIR), lambda i: (0, 0, i))] * 2,
        out_specs=pair_cols(L),
        out_shape=jax.ShapeDtypeStruct((L, D), F32),
        compiler_params=params(),
        cost_estimate=cost(1e6, 1e7),
        name="place_query",
    )(place, own, other)


def spread(blocks):
    return lax.all_to_all(blocks, ("seq", "dp"), split_axis=0, concat_axis=0, axis_index_groups=CORE_GROUPS)


def numer_x_kernel(place, n0, n1, n2, n3, s0, s1, s2, s3, fin, z0, z1, z2, z3, total):
    at = pl.ds(pl.multiple_of(place[0] * 256, 256), 256)
    for h in range(H):
        rows = slice(h * HD, (h + 1) * HD)
        pair, j = h // 2, h % 2
        acc = jnp.zeros((HD, 256), F32)
        for n, s in ((n0, s0), (n1, s1), (n2, s2), (n3, s3)):
            acc += n[rows, :] * jnp.exp2(s[pair, j : j + 1, at] - fin[pair, j : j + 1, at])
        total[rows, :] = acc
    for k, out in enumerate((z0, z1, z2, z3)):
        spot = lax.rem(place[1] + k, 4)
        row = pl.multiple_of(lax.rem(spot, 2) * 640, 640)
        lane = pl.multiple_of(lax.div(spot, 2) * 128, 128)
        out[...] = total[pl.ds(row, 640), pl.ds(lane, 128)]


def numer_z_kernel(z0, z1, z2, z3, out):
    out[...] = four(z0, z1, z2, z3).T


def round_kernel(x, out):
    for k in range(2):
        rows = slice(k * 128, (k + 1) * 128)
        out[rows, 0:640] = x[2 * k].astype(BF16)
        out[rows, 640:1280] = x[2 * k + 1].astype(BF16)


def after(first, values):
    return lax.optimization_barrier((first, values))[1]


def on_device(tokens, queries, key_weight, value_weight, out_grad):
    seq, dp = lax.axis_index("seq"), lax.axis_index("dp")
    place = jnp.stack([seq // 4, seq % 4, dp // 2, dp % 2]).astype(jnp.int32)
    grad = out_grad[0]

    keys, vals, normed, n0, n1, n2, n3, stats = forward(place, tokens[0], key_weight, value_weight, queries, grad)
    near = exchange([stats] * 4, "x")
    nt = reorder(row_order(place), normed)
    near, nt, n1, n2, n3 = lax.optimization_barrier((near, nt, n1, n2, n3))
    group = simple(merge_kernel, near, (PAIRS, 4, L), "merge")
    blocks = exchange([group] * 4, "z")
    numer = exchange([n0, n1, n2, n3], "x")
    fin = simple(merge_kernel, blocks, (PAIRS, 4, L), "finish")

    terms, q_terms = backward(nt, keys, vals, queries, grad, fin)
    q_cores = lax.all_to_all(q_terms, "dp", split_axis=0, concat_axis=0, axis_index_groups=PAIR_GROUPS)
    q_sum = q_cores[0] + q_cores[1]
    q_parts = spread(q_sum)
    numer, near = after(q_sum, (numer, near))
    rows = lax.psum_scatter(after(numer, terms), "dp", scatter_dimension=0, tiled=True)
    own_query = lax.all_to_all(
        query_sum(q_parts), ("seq", "dp"), split_axis=0, concat_axis=0, axis_index_groups=PLANE_GROUPS
    ).reshape(128, D)

    zs = simple(
        numer_x_kernel,
        [*numer, *near, fin],
        [(640, 128)] * 4,
        "numer_x",
        scalars=place,
        scratch=[pltpu.VMEM((D, 256), F32)],
        moved=7e6,
    )
    share = simple(numer_z_kernel, exchange(zs, "z"), (128, 640), "numer_z")
    gathered = lax.all_gather(after(q_parts, share), "seq")
    rows = after(own_query, rows)
    rows = exchange(simple(second_kernel, [rows], [(40, 2 * D)] * 4, "second"), "z")
    rows = simple(third_kernel, rows, [(16, 2 * D)] * 4, "third")
    own_query = jnp.stack(after(rows[0], exchange([own_query] * 4, "x")))
    rows = exchange(rows, "x")

    attended = pl.pallas_call(
        round_kernel,
        grid=(4,),
        in_specs=[pl.BlockSpec((4, 128, 640), lambda i: (i, 0, 0))],
        out_specs=pl.BlockSpec((256, D), lambda i: (i, 0)),
        out_shape=jax.ShapeDtypeStruct((L, D), BF16),
        compiler_params=params(),
        cost_estimate=cost(1e6, 8e6),
        name="round",
    )(gathered)
    other_query = after((attended, rows), shift(own_query, "c", 1))
    query_grad = place_query(place, own_query, other_query)
    key_rows, value_rows = simple(last_kernel, rows, [(10, D)] * 2, "last")
    return attended.reshape(1, L, D), query_grad, key_rows, value_rows


def solution(mesh):
    placed = (P("dp", "seq", None), P(), P(), P(), P("dp", None, None))
    return jax.shard_map(
        on_device,
        mesh=mesh,
        in_specs=placed,
        out_specs=(P("dp", None, None), P(), P(("seq", "dp"), None), P(("seq", "dp"), None)),
        check_vma=False,
    )
```

```python
import functools

import jax
import jax.numpy as jnp
import numpy as np
from jax import lax
from jax.experimental import pallas as pl
from jax.experimental.pallas import tpu as pltpu
from jax.sharding import PartitionSpec as P

H = 10
HD = 128
T = 512
L = 1024
D = 1280
PAIR = 2 * HD
SCALE = HD ** (-0.5)
SCALE2 = SCALE * 1.4426950408889634
VMEM_LIMIT = 56 * 1024 * 1024
PAIRS = H // 2
COST = 0.02
PAIR_GROUPS = [[a * 2, a * 2 + 1] for a in range(4)]
PLANE_GROUPS = [[a * 32 + b * 2 + c for b in range(16)] for a in range(4) for c in range(2)]
CORE_GROUPS = [[a * 2 + b for a in range(64)] for b in range(2)]
F32 = jnp.float32
BF16 = jnp.bfloat16


def shift(array, axis, step):
    if axis == "x":
        return lax.ppermute(array, "seq", [(a * 4 + b, (a + step) % 4 * 4 + b) for a in range(4) for b in range(4)])
    if axis == "z":
        return lax.ppermute(array, "seq", [(a * 4 + b, a * 4 + (b + step) % 4) for a in range(4) for b in range(4)])
    if axis == "y":
        return lax.ppermute(array, "dp", [(a * 2 + b, (a + step) % 4 * 2 + b) for a in range(4) for b in range(2)])
    return lax.ppermute(array, "dp", [(a * 2 + b, a * 2 + 1 - b) for a in range(4) for b in range(2)])


def nt_dot(a, b):
    return lax.dot_general(a, b, (((1,), (1,)), ((), ())), preferred_element_type=F32)


def dot(a, b):
    return jnp.dot(a, b, preferred_element_type=F32)


def params():
    return pltpu.CompilerParams(vmem_limit_bytes=VMEM_LIMIT)


def cost(flops, moved):
    return pl.CostEstimate(flops=int(flops * COST), bytes_accessed=int(moved * COST), transcendentals=0)


def full(shape):
    return pl.BlockSpec(shape, lambda *_: (0,) * len(shape))


SMEM = pl.BlockSpec(memory_space=pltpu.SMEM)


def forward_kernel(place, tok, kw, vw, q, g, k_out, v_out, normed_out, n0, n1, n2, n3, stats, normed, s, w, numer):
    @pl.when(pl.program_id(0) == 0)
    def _():
        values = tok[...].astype(F32)
        centre = values - jnp.mean(values, axis=-1, keepdims=True)
        spread = jnp.mean(centre * centre, axis=-1, keepdims=True)
        normed[...] = (centre * lax.rsqrt(spread + 1e-05)).astype(BF16)
        normed_out[...] = normed[...]

    keys = dot(normed[...], kw[...]).astype(BF16)
    vals = dot(normed[...], vw[...]).astype(BF16)
    k_out[...] = keys
    v_out[...] = vals
    vals_t = vals.T
    grad_t = g[...].T
    for j in range(2):
        head = slice(j * HD, (j + 1) * HD)
        tops, totals = [], []
        for tile in range(L // 256):
            at = slice(tile * 256, (tile + 1) * 256)
            scores = nt_dot(keys[:, head], q[at, head])
            high = jnp.max(scores, axis=0, keepdims=True) * SCALE2
            shifted = jnp.exp2(scores * SCALE2 - high)
            tops.append(high)
            totals.append(jnp.sum(shifted, axis=0, keepdims=True))
            w[j, :, at] = shifted.astype(BF16)
        total = jnp.concatenate(totals, axis=1)
        part = dot(vals_t[head, :], w[j]) * (1.0 / total)
        numer[head, :] = part
        stats[0, j : j + 1, :] = jnp.concatenate(tops, axis=1) + jnp.log2(total)
        stats[0, 2 + j : 3 + j, :] = jnp.sum(part * grad_t[head, :].astype(F32), axis=0, keepdims=True)
    for k, out in enumerate((n0, n1, n2, n3)):
        start = pl.multiple_of(lax.rem(place[0] + k, 4) * 256, 256)
        out[...] = numer[:, pl.ds(start, 256)]


def forward(place, tokens, kw, vw, q, g):
    cols = lambda rows: pl.BlockSpec((rows, PAIR), lambda i: (0, i))
    return pl.pallas_call(
        forward_kernel,
        grid=(PAIRS,),
        in_specs=[SMEM, full((T, D)), cols(D), cols(D), cols(L), cols(L)],
        out_specs=[cols(T), cols(T), full((T, D))]
        + [pl.BlockSpec((PAIR, 256), lambda i: (i, 0))] * 4
        + [pl.BlockSpec((1, 4, L), lambda i: (i, 0, 0))],
        out_shape=[jax.ShapeDtypeStruct((T, D), BF16)] * 3
        + [jax.ShapeDtypeStruct((D, 256), F32)] * 4
        + [jax.ShapeDtypeStruct((PAIRS, 4, L), F32)],
        scratch_shapes=[
            pltpu.VMEM((T, D), BF16),
            pltpu.VMEM((2, T, L), F32),
            pltpu.VMEM((2, T, L), BF16),
            pltpu.VMEM((PAIR, L), F32),
        ],
        compiler_params=params(),
        cost_estimate=cost(1.2e10, 2.4e7),
        name="forward",
    )(place, tokens, kw, vw, q, g)


def merge_kernel(s0, s1, s2, s3, out):
    blocks = (s0, s1, s2, s3)
    top = functools.reduce(jnp.maximum, [b[:, 0:2, :] for b in blocks])
    total = jnp.zeros_like(top)
    inner = jnp.zeros_like(top)
    for b in blocks:
        factor = jnp.exp2(b[:, 0:2, :] - top)
        total += factor
        inner += b[:, 2:4, :] * factor
    out[:, 0:2, :] = top + jnp.log2(total)
    out[:, 2:4, :] = inner / total


def simple(kernel, ins, outs, name, scalars=None, scratch=(), moved=4e6, flops=1e6):
    specs = [pl.BlockSpec(memory_space=pltpu.VMEM)] * len(ins)
    several = isinstance(outs, list)
    shapes = [jax.ShapeDtypeStruct(o, F32) for o in (outs if several else [outs])]
    return pl.pallas_call(
        kernel,
        in_specs=([] if scalars is None else [SMEM]) + specs,
        out_shape=shapes if several else shapes[0],
        scratch_shapes=list(scratch),
        compiler_params=params(),
        cost_estimate=cost(flops, moved),
        name=name,
    )(*([] if scalars is None else [scalars]), *ins)


def reorder_kernel(order, normed, out):
    feature = lax.broadcasted_iota(jnp.int32, (D, D), 0)
    choose = jnp.where(feature == order[...], 1.0, 0.0).astype(BF16)
    out[...] = dot(normed[...], choose).astype(BF16).T


def reorder(order, normed):
    return pl.pallas_call(
        reorder_kernel,
        out_shape=jax.ShapeDtypeStruct((D, T), BF16),
        compiler_params=params(),
        cost_estimate=cost(2 * T * D * D, 3e6),
        name="reorder",
    )(order, normed)


def row_order(place):
    digits = [jnp.asarray(d, jnp.int32) for d in np.indices((4, 2, 4, 4, 10)).reshape(5, D)]
    z = (place[1] + digits[2]) % 4
    x = (place[0] + digits[3]) % 4
    owner = ((x * 4 + z) * 4 + digits[0]) * 2 + digits[1]
    return (owner * 10 + digits[4]).reshape(1, D)


def pair_cols(rows):
    return pl.BlockSpec((rows, PAIR), lambda i: (0, i))


def backward_kernel(nt, keys, vals, q, g, fin, out, q_out, s, pg, p, sg, kgrad, vgrad):
    keys_t = keys[...].T
    for j in range(2):
        head = slice(j * HD, (j + 1) * HD)
        for tile in range(L // 256):
            at = slice(tile * 256, (tile + 1) * 256)
            probs = jnp.exp2(nt_dot(keys[:, head], q[at, head]) * SCALE2 - fin[0, j : j + 1, at])
            p[j, :, at] = probs.astype(BF16)
            sg[j, :, at] = (probs * (nt_dot(vals[:, head], g[at, head]) - fin[0, 2 + j : 3 + j, at]) * SCALE).astype(BF16)
        query = dot(keys_t[head, :], sg[j]).T
        q_out[:, :, :, head] = query.reshape(2, 64, 8, HD)
        kgrad[:, head] = dot(sg[j], q[:, head]).astype(BF16)
        vgrad[:, head] = dot(p[j], g[:, head]).astype(BF16)
    out[:, 0:PAIR] = dot(nt[...], kgrad[...])
    out[:, PAIR:] = dot(nt[...], vgrad[...])


def backward(nt, keys, vals, q, g, fin):
    return pl.pallas_call(
        backward_kernel,
        grid=(PAIRS,),
        in_specs=[
            full((D, T)),
            pair_cols(T),
            pair_cols(T),
            pair_cols(L),
            pair_cols(L),
            pl.BlockSpec((1, 4, L), lambda i: (i, 0, 0)),
        ],
        out_specs=[
            pl.BlockSpec((D, 2 * PAIR), lambda i: (0, i)),
            pl.BlockSpec((2, 64, 8, PAIR), lambda i: (0, 0, 0, i)),
        ],
        out_shape=[jax.ShapeDtypeStruct((D, 2 * D), F32), jax.ShapeDtypeStruct((2, 64, 8, D), F32)],
        scratch_shapes=[
            pltpu.VMEM((2, T, L), F32),
            pltpu.VMEM((2, T, L), F32),
            pltpu.VMEM((2, T, L), BF16),
            pltpu.VMEM((2, T, L), BF16),
            pltpu.VMEM((T, PAIR), BF16),
            pltpu.VMEM((T, PAIR), BF16),
        ],
        compiler_params=params(),
        cost_estimate=cost(2e10, 3.0e7),
        name="backward",
    )(nt, keys, vals, q, g, fin)


def four(a0, a1, a2, a3):
    return (a0[...] + a2[...]) + (a1[...] + a3[...])


def exchange(chunks, axis):
    far = {k: shift(chunks[k], axis, k) for k in (2, 1, 3)}
    return [chunks[0], far[1], far[2], far[3]]


def second_kernel(rows, *outs):
    for k, out in enumerate(outs):
        out[...] = rows[k * 40 : (k + 1) * 40]


def third_kernel(a0, a1, a2, a3, *outs):
    rows = four(a0, a1, a2, a3)
    for k, out in enumerate(outs):
        out[0:10, :] = rows[k * 10 : (k + 1) * 10]
        out[10:16, :] = jnp.zeros((6, 2 * D), F32)


def last_kernel(a0, a1, a2, a3, key_rows, value_rows):
    rows = four(a0, a1, a2, a3)
    for i in range(PAIRS):
        cols = slice(i * PAIR, (i + 1) * PAIR)
        key_rows[:, cols] = rows[0:10, 2 * i * PAIR : (2 * i + 1) * PAIR]
        value_rows[:, cols] = rows[0:10, (2 * i + 1) * PAIR : (2 * i + 2) * PAIR]


def query_sum_kernel(parts, out):
    rows = parts[0]
    for k in range(1, 64):
        rows += parts[k]
    for k in range(16):
        out[k] = rows


def query_sum(parts):
    return simple(query_sum_kernel, [parts], (16, 8, D), "query_sum")


def place_query_kernel(place, rows, *refs):
    refs[-1][...] = rows[0]


def place_query(place, rows, before=None):
    def spot(k, p):
        half = p[3] if before is None else 1 - p[3]
        return half * 4 + lax.rem(p[0] + 4 - k, 4), 0

    others = [] if before is None else [before]
    return pl.pallas_call(
        place_query_kernel,
        grid_spec=pltpu.PrefetchScalarGridSpec(
            num_scalar_prefetch=1,
            grid=(4,),
            in_specs=[pl.BlockSpec((1, 128, D), lambda k, p: (k, 0, 0))] + [pl.BlockSpec(memory_space=pl.ANY)] * len(others),
            out_specs=pl.BlockSpec((128, D), spot),
        ),
        out_shape=jax.ShapeDtypeStruct((L, D), F32),
        input_output_aliases={} if before is None else {2: 0},
        compiler_params=params(),
        cost_estimate=cost(1e6, 6e6),
        name="place_query",
    )(place, rows, *others)


def spread(blocks):
    return lax.all_to_all(blocks, ("seq", "dp"), split_axis=0, concat_axis=0, axis_index_groups=CORE_GROUPS)


def numer_x_kernel(place, n0, n1, n2, n3, s0, s1, s2, s3, fin, z0, z1, z2, z3, total):
    at = pl.ds(pl.multiple_of(place[0] * 256, 256), 256)
    for h in range(H):
        rows = slice(h * HD, (h + 1) * HD)
        pair, j = h // 2, h % 2
        acc = jnp.zeros((HD, 256), F32)
        for n, s in ((n0, s0), (n1, s1), (n2, s2), (n3, s3)):
            acc += n[rows, :] * jnp.exp2(s[pair, j : j + 1, at] - fin[pair, j : j + 1, at])
        total[rows, :] = acc
    for k, out in enumerate((z0, z1, z2, z3)):
        spot = lax.rem(place[1] + k, 4)
        row = pl.multiple_of(lax.rem(spot, 2) * 640, 640)
        lane = pl.multiple_of(lax.div(spot, 2) * 128, 128)
        out[...] = total[pl.ds(row, 640), pl.ds(lane, 128)]


def numer_z_kernel(z0, z1, z2, z3, out):
    out[...] = four(z0, z1, z2, z3).T


def round_kernel(x, out):
    for k in range(2):
        rows = slice(k * 128, (k + 1) * 128)
        out[rows, 0:640] = x[2 * k].astype(BF16)
        out[rows, 640:1280] = x[2 * k + 1].astype(BF16)


def after(first, values):
    return lax.optimization_barrier((first, values))[1]


def on_device(tokens, queries, key_weight, value_weight, out_grad):
    seq, dp = lax.axis_index("seq"), lax.axis_index("dp")
    place = jnp.stack([seq // 4, seq % 4, dp // 2, dp % 2]).astype(jnp.int32)
    grad = out_grad[0]

    keys, vals, normed, n0, n1, n2, n3, stats = forward(place, tokens[0], key_weight, value_weight, queries, grad)
    near = exchange([stats] * 4, "x")
    nt = reorder(row_order(place), normed)
    near, nt, n1, n2, n3 = lax.optimization_barrier((near, nt, n1, n2, n3))
    group = simple(merge_kernel, near, (PAIRS, 4, L), "merge")
    blocks = exchange([group] * 4, "z")
    numer = exchange([n0, n1, n2, n3], "x")
    fin = simple(merge_kernel, blocks, (PAIRS, 4, L), "finish")

    terms, q_terms = backward(nt, keys, vals, queries, grad, fin)
    q_cores = lax.all_to_all(q_terms, "dp", split_axis=0, concat_axis=0, axis_index_groups=PAIR_GROUPS)
    q_sum = q_cores[0] + q_cores[1]
    q_parts = spread(q_sum)
    numer, near = after(q_sum, (numer, near))
    rows = lax.psum_scatter(after(numer, terms), "dp", scatter_dimension=0, tiled=True)
    own_query = lax.all_to_all(
        query_sum(q_parts), ("seq", "dp"), split_axis=0, concat_axis=0, axis_index_groups=PLANE_GROUPS
    ).reshape(128, D)

    zs = simple(
        numer_x_kernel,
        [*numer, *near, fin],
        [(640, 128)] * 4,
        "numer_x",
        scalars=place,
        scratch=[pltpu.VMEM((D, 256), F32)],
        moved=7e6,
    )
    share = simple(numer_z_kernel, exchange(zs, "z"), (128, 640), "numer_z")
    gathered = lax.all_gather(after(q_parts, share), "seq")
    right, left = shift(own_query, "x", 1), shift(own_query, "x", 3)
    rows = after((right, left), rows)
    rows = exchange(simple(second_kernel, [rows], [(40, 2 * D)] * 4, "second"), "z")
    rows = simple(third_kernel, rows, [(16, 2 * D)] * 4, "third")
    own_query = jnp.stack([own_query, right, after(rows[0], shift(own_query, "x", 2)), left])
    rows = exchange(rows, "x")

    attended = pl.pallas_call(
        round_kernel,
        grid=(4,),
        in_specs=[pl.BlockSpec((4, 128, 640), lambda i: (i, 0, 0))],
        out_specs=pl.BlockSpec((256, D), lambda i: (i, 0)),
        out_shape=jax.ShapeDtypeStruct((L, D), BF16),
        compiler_params=params(),
        cost_estimate=cost(1e6, 8e6),
        name="round",
    )(gathered)
    half_placed = place_query(place, own_query)
    other_query = after((attended, rows, half_placed), shift(own_query, "c", 1))
    query_grad = place_query(place, other_query, half_placed)
    key_rows, value_rows = simple(last_kernel, rows, [(10, D)] * 2, "last")
    return attended.reshape(1, L, D), query_grad, key_rows, value_rows


def solution(mesh):
    placed = (P("dp", "seq", None), P(), P(), P(), P("dp", None, None))
    return jax.shard_map(
        on_device,
        mesh=mesh,
        in_specs=placed,
        out_specs=(P("dp", None, None), P(), P(("seq", "dp"), None), P(("seq", "dp"), None)),
        check_vma=False,
    )
```

```python
import functools

import jax
import jax.numpy as jnp
import numpy as np
from jax import lax
from jax.experimental import pallas as pl
from jax.experimental.pallas import tpu as pltpu
from jax.sharding import PartitionSpec as P

H = 10
HD = 128
T = 512
L = 1024
D = 1280
PAIR = 2 * HD
SCALE = HD ** (-0.5)
SCALE2 = SCALE * 1.4426950408889634
VMEM_LIMIT = 56 * 1024 * 1024
PAIRS = H // 2
COST = 0.02
PAIR_GROUPS = [[a * 2, a * 2 + 1] for a in range(4)]
PLANE_GROUPS = [[a * 32 + b * 2 + c for b in range(16)] for a in range(4) for c in range(2)]
CORE_GROUPS = [[a * 2 + b for a in range(64)] for b in range(2)]
F32 = jnp.float32
BF16 = jnp.bfloat16


def shift(array, axis, step):
    if axis == "x":
        return lax.ppermute(array, "seq", [(a * 4 + b, (a + step) % 4 * 4 + b) for a in range(4) for b in range(4)])
    if axis == "z":
        return lax.ppermute(array, "seq", [(a * 4 + b, a * 4 + (b + step) % 4) for a in range(4) for b in range(4)])
    if axis == "y":
        return lax.ppermute(array, "dp", [(a * 2 + b, (a + step) % 4 * 2 + b) for a in range(4) for b in range(2)])
    return lax.ppermute(array, "dp", [(a * 2 + b, a * 2 + 1 - b) for a in range(4) for b in range(2)])


def nt_dot(a, b):
    return lax.dot_general(a, b, (((1,), (1,)), ((), ())), preferred_element_type=F32)


def dot(a, b):
    return jnp.dot(a, b, preferred_element_type=F32)


def params():
    return pltpu.CompilerParams(vmem_limit_bytes=VMEM_LIMIT)


def cost(flops, moved):
    return pl.CostEstimate(flops=int(flops * COST), bytes_accessed=int(moved * COST), transcendentals=0)


def full(shape):
    return pl.BlockSpec(shape, lambda *_: (0,) * len(shape))


SMEM = pl.BlockSpec(memory_space=pltpu.SMEM)


def forward_kernel(place, tok, kw, vw, q, g, k_out, v_out, normed_out, n0, n1, n2, n3, stats, normed, s, w, numer):
    @pl.when(pl.program_id(0) == 0)
    def _():
        values = tok[...].astype(F32)
        centre = values - jnp.mean(values, axis=-1, keepdims=True)
        spread = jnp.mean(centre * centre, axis=-1, keepdims=True)
        normed[...] = (centre * lax.rsqrt(spread + 1e-05)).astype(BF16)
        normed_out[...] = normed[...]

    keys = dot(normed[...], kw[...]).astype(BF16)
    vals = dot(normed[...], vw[...]).astype(BF16)
    k_out[...] = keys
    v_out[...] = vals
    vals_t = vals.T
    grad_t = g[...].T
    for j in range(2):
        head = slice(j * HD, (j + 1) * HD)
        tops, totals = [], []
        for tile in range(L // 256):
            at = slice(tile * 256, (tile + 1) * 256)
            scores = nt_dot(keys[:, head], q[at, head])
            high = jnp.max(scores, axis=0, keepdims=True) * SCALE2
            shifted = jnp.exp2(scores * SCALE2 - high)
            tops.append(high)
            totals.append(jnp.sum(shifted, axis=0, keepdims=True))
            w[j, :, at] = shifted.astype(BF16)
        total = jnp.concatenate(totals, axis=1)
        part = dot(vals_t[head, :], w[j]) * (1.0 / total)
        numer[head, :] = part
        stats[0, j : j + 1, :] = jnp.concatenate(tops, axis=1) + jnp.log2(total)
        stats[0, 2 + j : 3 + j, :] = jnp.sum(part * grad_t[head, :].astype(F32), axis=0, keepdims=True)
    for k, out in enumerate((n0, n1, n2, n3)):
        start = pl.multiple_of(lax.rem(place[0] + k, 4) * 256, 256)
        out[...] = numer[:, pl.ds(start, 256)]


def forward(place, tokens, kw, vw, q, g):
    cols = lambda rows: pl.BlockSpec((rows, PAIR), lambda i: (0, i))
    return pl.pallas_call(
        forward_kernel,
        grid=(PAIRS,),
        in_specs=[SMEM, full((T, D)), cols(D), cols(D), cols(L), cols(L)],
        out_specs=[cols(T), cols(T), full((T, D))]
        + [pl.BlockSpec((PAIR, 256), lambda i: (i, 0))] * 4
        + [pl.BlockSpec((1, 4, L), lambda i: (i, 0, 0))],
        out_shape=[jax.ShapeDtypeStruct((T, D), BF16)] * 3
        + [jax.ShapeDtypeStruct((D, 256), F32)] * 4
        + [jax.ShapeDtypeStruct((PAIRS, 4, L), F32)],
        scratch_shapes=[
            pltpu.VMEM((T, D), BF16),
            pltpu.VMEM((2, T, L), F32),
            pltpu.VMEM((2, T, L), BF16),
            pltpu.VMEM((PAIR, L), F32),
        ],
        compiler_params=params(),
        cost_estimate=cost(1.2e10, 2.4e7),
        name="forward",
    )(place, tokens, kw, vw, q, g)


def merge_kernel(s0, s1, s2, s3, out):
    blocks = (s0, s1, s2, s3)
    top = functools.reduce(jnp.maximum, [b[:, 0:2, :] for b in blocks])
    total = jnp.zeros_like(top)
    inner = jnp.zeros_like(top)
    for b in blocks:
        factor = jnp.exp2(b[:, 0:2, :] - top)
        total += factor
        inner += b[:, 2:4, :] * factor
    out[:, 0:2, :] = top + jnp.log2(total)
    out[:, 2:4, :] = inner / total


def simple(kernel, ins, outs, name, scalars=None, scratch=(), moved=4e6, flops=1e6):
    specs = [pl.BlockSpec(memory_space=pltpu.VMEM)] * len(ins)
    several = isinstance(outs, list)
    shapes = [jax.ShapeDtypeStruct(o, F32) for o in (outs if several else [outs])]
    return pl.pallas_call(
        kernel,
        in_specs=([] if scalars is None else [SMEM]) + specs,
        out_shape=shapes if several else shapes[0],
        scratch_shapes=list(scratch),
        compiler_params=params(),
        cost_estimate=cost(flops, moved),
        name=name,
    )(*([] if scalars is None else [scalars]), *ins)


def reorder_kernel(order, normed, out):
    feature = lax.broadcasted_iota(jnp.int32, (D, D), 0)
    choose = jnp.where(feature == order[...], 1.0, 0.0).astype(BF16)
    out[...] = dot(normed[...], choose).astype(BF16).T


def reorder(order, normed):
    return pl.pallas_call(
        reorder_kernel,
        out_shape=jax.ShapeDtypeStruct((D, T), BF16),
        compiler_params=params(),
        cost_estimate=cost(2 * T * D * D, 3e6),
        name="reorder",
    )(order, normed)


def row_order(place):
    digits = [jnp.asarray(d, jnp.int32) for d in np.indices((4, 2, 4, 4, 10)).reshape(5, D)]
    z = (place[1] + digits[2]) % 4
    x = (place[0] + digits[3]) % 4
    owner = ((x * 4 + z) * 4 + digits[0]) * 2 + digits[1]
    return (owner * 10 + digits[4]).reshape(1, D)


def pair_cols(rows):
    return pl.BlockSpec((rows, PAIR), lambda i: (0, i))


def backward_kernel(nt, keys, vals, q, g, fin, out, q_out, s, pg, p, sg, kgrad, vgrad):
    keys_t = keys[...].T
    for j in range(2):
        head = slice(j * HD, (j + 1) * HD)
        for tile in range(L // 256):
            at = slice(tile * 256, (tile + 1) * 256)
            probs = jnp.exp2(nt_dot(keys[:, head], q[at, head]) * SCALE2 - fin[0, j : j + 1, at])
            p[j, :, at] = probs.astype(BF16)
            sg[j, :, at] = (probs * (nt_dot(vals[:, head], g[at, head]) - fin[0, 2 + j : 3 + j, at]) * SCALE).astype(BF16)
        query = dot(keys_t[head, :], sg[j]).T
        q_out[:, :, :, head] = query.reshape(2, 64, 8, HD)
        kgrad[:, head] = dot(sg[j], q[:, head]).astype(BF16)
        vgrad[:, head] = dot(p[j], g[:, head]).astype(BF16)
    out[:, 0:PAIR] = dot(nt[...], kgrad[...])
    out[:, PAIR:] = dot(nt[...], vgrad[...])


def backward(nt, keys, vals, q, g, fin):
    return pl.pallas_call(
        backward_kernel,
        grid=(PAIRS,),
        in_specs=[
            full((D, T)),
            pair_cols(T),
            pair_cols(T),
            pair_cols(L),
            pair_cols(L),
            pl.BlockSpec((1, 4, L), lambda i: (i, 0, 0)),
        ],
        out_specs=[
            pl.BlockSpec((D, 2 * PAIR), lambda i: (0, i)),
            pl.BlockSpec((2, 64, 8, PAIR), lambda i: (0, 0, 0, i)),
        ],
        out_shape=[jax.ShapeDtypeStruct((D, 2 * D), F32), jax.ShapeDtypeStruct((2, 64, 8, D), F32)],
        scratch_shapes=[
            pltpu.VMEM((2, T, L), F32),
            pltpu.VMEM((2, T, L), F32),
            pltpu.VMEM((2, T, L), BF16),
            pltpu.VMEM((2, T, L), BF16),
            pltpu.VMEM((T, PAIR), BF16),
            pltpu.VMEM((T, PAIR), BF16),
        ],
        compiler_params=params(),
        cost_estimate=cost(2e10, 3.0e7),
        name="backward",
    )(nt, keys, vals, q, g, fin)


def four(a0, a1, a2, a3):
    return (a0[...] + a2[...]) + (a1[...] + a3[...])


def exchange(chunks, axis):
    far = {k: shift(chunks[k], axis, k) for k in (2, 1, 3)}
    return [chunks[0], far[1], far[2], far[3]]


def second_kernel(rows, *outs):
    for k, out in enumerate(outs):
        out[...] = rows[k * 40 : (k + 1) * 40]


def third_kernel(a0, a1, a2, a3, *outs):
    rows = four(a0, a1, a2, a3)
    for k, out in enumerate(outs):
        out[0:10, :] = rows[k * 10 : (k + 1) * 10]
        out[10:16, :] = jnp.zeros((6, 2 * D), F32)


def last_kernel(a0, a1, a2, a3, key_rows, value_rows):
    rows = four(a0, a1, a2, a3)
    for i in range(PAIRS):
        cols = slice(i * PAIR, (i + 1) * PAIR)
        key_rows[:, cols] = rows[0:10, 2 * i * PAIR : (2 * i + 1) * PAIR]
        value_rows[:, cols] = rows[0:10, (2 * i + 1) * PAIR : (2 * i + 2) * PAIR]


def query_sum_kernel(parts, out):
    rows = parts[0]
    for k in range(1, 64):
        rows += parts[k]
    for k in range(16):
        out[k] = rows


def query_sum(parts):
    return simple(query_sum_kernel, [parts], (16, 8, D), "query_sum")


def place_query_kernel(hops, place, own, other, *refs):
    out, sems = refs[-2], refs[-1]
    copies = []
    for i, hop in enumerate(hops):
        block = lax.rem(place[0] + 4 - hop, 4) * 128
        for j, (half, rows) in enumerate(((place[3], own), (1 - place[3], other))):
            start = pl.multiple_of(half * 512 + block, 128)
            copies.append(pltpu.make_async_copy(rows.at[i], out.at[pl.ds(start, 128)], sems.at[2 * i + j]))
    for copy in copies:
        copy.start()
    for copy in copies:
        copy.wait()


def place_query(place, hops, own, other, before=None):
    arrays = [own, other] + ([] if before is None else [before])
    return pl.pallas_call(
        functools.partial(place_query_kernel, hops),
        in_specs=[SMEM] + [pl.BlockSpec(memory_space=pl.ANY)] * len(arrays),
        out_specs=pl.BlockSpec(memory_space=pl.ANY),
        out_shape=jax.ShapeDtypeStruct((L, D), F32),
        input_output_aliases={} if before is None else {3: 0},
        scratch_shapes=[pltpu.SemaphoreType.DMA((2 * len(hops),))],
        compiler_params=params(),
        cost_estimate=cost(1e6, 6e6),
        name="place_query",
    )(place, *arrays)


def spread(blocks):
    return lax.all_to_all(blocks, ("seq", "dp"), split_axis=0, concat_axis=0, axis_index_groups=CORE_GROUPS)


def numer_x_kernel(place, n0, n1, n2, n3, s0, s1, s2, s3, fin, z0, z1, z2, z3, total):
    at = pl.ds(pl.multiple_of(place[0] * 256, 256), 256)
    for h in range(H):
        rows = slice(h * HD, (h + 1) * HD)
        pair, j = h // 2, h % 2
        acc = jnp.zeros((HD, 256), F32)
        for n, s in ((n0, s0), (n1, s1), (n2, s2), (n3, s3)):
            acc += n[rows, :] * jnp.exp2(s[pair, j : j + 1, at] - fin[pair, j : j + 1, at])
        total[rows, :] = acc
    for k, out in enumerate((z0, z1, z2, z3)):
        spot = lax.rem(place[1] + k, 4)
        row = pl.multiple_of(lax.rem(spot, 2) * 640, 640)
        lane = pl.multiple_of(lax.div(spot, 2) * 128, 128)
        out[...] = total[pl.ds(row, 640), pl.ds(lane, 128)]


def numer_z_kernel(z0, z1, z2, z3, out):
    out[...] = four(z0, z1, z2, z3).T


def round_kernel(x, out):
    for k in range(2):
        rows = slice(k * 128, (k + 1) * 128)
        out[rows, 0:640] = x[2 * k].astype(BF16)
        out[rows, 640:1280] = x[2 * k + 1].astype(BF16)


def after(first, values):
    return lax.optimization_barrier((first, values))[1]


def on_device(tokens, queries, key_weight, value_weight, out_grad):
    seq, dp = lax.axis_index("seq"), lax.axis_index("dp")
    place = jnp.stack([seq // 4, seq % 4, dp // 2, dp % 2]).astype(jnp.int32)
    grad = out_grad[0]

    keys, vals, normed, n0, n1, n2, n3, stats = forward(place, tokens[0], key_weight, value_weight, queries, grad)
    near = exchange([stats] * 4, "x")
    nt = reorder(row_order(place), normed)
    near, nt, n1, n2, n3 = lax.optimization_barrier((near, nt, n1, n2, n3))
    group = simple(merge_kernel, near, (PAIRS, 4, L), "merge")
    blocks = exchange([group] * 4, "z")
    numer = exchange([n0, n1, n2, n3], "x")
    fin = simple(merge_kernel, blocks, (PAIRS, 4, L), "finish")

    terms, q_terms = backward(nt, keys, vals, queries, grad, fin)
    q_cores = lax.all_to_all(q_terms, "dp", split_axis=0, concat_axis=0, axis_index_groups=PAIR_GROUPS)
    q_sum = q_cores[0] + q_cores[1]
    q_parts = spread(q_sum)
    numer, near = after(q_sum, (numer, near))
    rows = lax.psum_scatter(after(numer, terms), "dp", scatter_dimension=0, tiled=True)
    own_query = lax.all_to_all(
        query_sum(q_parts), ("seq", "dp"), split_axis=0, concat_axis=0, axis_index_groups=PLANE_GROUPS
    ).reshape(128, D)

    zs = simple(
        numer_x_kernel,
        [*numer, *near, fin],
        [(640, 128)] * 4,
        "numer_x",
        scalars=place,
        scratch=[pltpu.VMEM((D, 256), F32)],
        moved=7e6,
    )
    share = simple(numer_z_kernel, exchange(zs, "z"), (128, 640), "numer_z")
    gathered = lax.all_gather(after(q_parts, share), "seq")
    right, left = shift(own_query, "x", 1), shift(own_query, "x", 3)
    rows = after((right, left), rows)
    far = shift(own_query, "x", 2)
    rows = exchange(simple(second_kernel, [rows], [(40, 2 * D)] * 4, "second"), "z")
    near_query = jnp.stack([own_query, right, left])
    query_grad = place_query(place, (0, 1, 3), near_query, shift(near_query, "c", 1))
    rows = simple(third_kernel, after(query_grad, rows), [(16, 2 * D)] * 4, "third")
    far = after(rows[0], far).reshape(1, 128, D)
    rows = exchange(rows, "x")

    attended = pl.pallas_call(
        round_kernel,
        grid=(4,),
        in_specs=[pl.BlockSpec((4, 128, 640), lambda i: (i, 0, 0))],
        out_specs=pl.BlockSpec((256, D), lambda i: (i, 0)),
        out_shape=jax.ShapeDtypeStruct((L, D), BF16),
        compiler_params=params(),
        cost_estimate=cost(1e6, 8e6),
        name="round",
    )(gathered)
    far_other = after(attended, shift(far, "c", 1))
    query_grad = place_query(place, (2,), far, far_other, query_grad)
    key_rows, value_rows = simple(last_kernel, rows, [(10, D)] * 2, "last")
    return attended.reshape(1, L, D), query_grad, key_rows, value_rows


def solution(mesh):
    placed = (P("dp", "seq", None), P(), P(), P(), P("dp", None, None))
    return jax.shard_map(
        on_device,
        mesh=mesh,
        in_specs=placed,
        out_specs=(P("dp", None, None), P(), P(("seq", "dp"), None), P(("seq", "dp"), None)),
        check_vma=False,
    )
```

```python
import functools

import jax
import jax.numpy as jnp
import numpy as np
from jax import lax
from jax.experimental import pallas as pl
from jax.experimental.pallas import tpu as pltpu
from jax.sharding import PartitionSpec as P

H = 10
HD = 128
T = 512
L = 1024
D = 1280
PAIR = 2 * HD
SCALE = HD ** (-0.5)
SCALE2 = SCALE * 1.4426950408889634
VMEM_LIMIT = 56 * 1024 * 1024
PAIRS = H // 2
COST = 0.02
PAIR_GROUPS = [[a * 2, a * 2 + 1] for a in range(4)]
PLANE_GROUPS = [[a * 32 + b * 2 + c for b in range(16)] for a in range(4) for c in range(2)]
CORE_GROUPS = [[a * 2 + b for a in range(64)] for b in range(2)]
F32 = jnp.float32
BF16 = jnp.bfloat16


def shift(array, axis, step):
    if axis == "x":
        return lax.ppermute(array, "seq", [(a * 4 + b, (a + step) % 4 * 4 + b) for a in range(4) for b in range(4)])
    if axis == "z":
        return lax.ppermute(array, "seq", [(a * 4 + b, a * 4 + (b + step) % 4) for a in range(4) for b in range(4)])
    if axis == "y":
        return lax.ppermute(array, "dp", [(a * 2 + b, (a + step) % 4 * 2 + b) for a in range(4) for b in range(2)])
    return lax.ppermute(array, "dp", [(a * 2 + b, a * 2 + 1 - b) for a in range(4) for b in range(2)])


def nt_dot(a, b):
    return lax.dot_general(a, b, (((1,), (1,)), ((), ())), preferred_element_type=F32)


def dot(a, b):
    return jnp.dot(a, b, preferred_element_type=F32)


def params():
    return pltpu.CompilerParams(vmem_limit_bytes=VMEM_LIMIT)


def cost(flops, moved):
    return pl.CostEstimate(flops=int(flops * COST), bytes_accessed=int(moved * COST), transcendentals=0)


def full(shape):
    return pl.BlockSpec(shape, lambda *_: (0,) * len(shape))


SMEM = pl.BlockSpec(memory_space=pltpu.SMEM)


def forward_kernel(place, tok, kw, vw, q, g, k_out, v_out, normed_out, n0, n1, n2, n3, stats, normed, s, w, numer):
    @pl.when(pl.program_id(0) == 0)
    def _():
        values = tok[...].astype(F32)
        centre = values - jnp.mean(values, axis=-1, keepdims=True)
        spread = jnp.mean(centre * centre, axis=-1, keepdims=True)
        normed[...] = (centre * lax.rsqrt(spread + 1e-05)).astype(BF16)
        normed_out[...] = normed[...]

    keys = dot(normed[...], kw[...]).astype(BF16)
    vals = dot(normed[...], vw[...]).astype(BF16)
    k_out[...] = keys
    v_out[...] = vals
    vals_t = vals.T
    grad_t = g[...].T
    for j in range(2):
        head = slice(j * HD, (j + 1) * HD)
        tops, totals = [], []
        for tile in range(L // 256):
            at = slice(tile * 256, (tile + 1) * 256)
            scores = nt_dot(keys[:, head], q[at, head])
            high = jnp.max(scores, axis=0, keepdims=True) * SCALE2
            shifted = jnp.exp2(scores * SCALE2 - high)
            tops.append(high)
            totals.append(jnp.sum(shifted, axis=0, keepdims=True))
            w[j, :, at] = shifted.astype(BF16)
        total = jnp.concatenate(totals, axis=1)
        part = dot(vals_t[head, :], w[j]) * (1.0 / total)
        numer[head, :] = part
        stats[0, j : j + 1, :] = jnp.concatenate(tops, axis=1) + jnp.log2(total)
        stats[0, 2 + j : 3 + j, :] = jnp.sum(part * grad_t[head, :].astype(F32), axis=0, keepdims=True)
    for k, out in enumerate((n0, n1, n2, n3)):
        start = pl.multiple_of(lax.rem(place[0] + k, 4) * 256, 256)
        out[...] = numer[:, pl.ds(start, 256)]


def forward(place, tokens, kw, vw, q, g):
    cols = lambda rows: pl.BlockSpec((rows, PAIR), lambda i: (0, i))
    return pl.pallas_call(
        forward_kernel,
        grid=(PAIRS,),
        in_specs=[SMEM, full((T, D)), cols(D), cols(D), cols(L), cols(L)],
        out_specs=[cols(T), cols(T), full((T, D))]
        + [pl.BlockSpec((PAIR, 256), lambda i: (i, 0))] * 4
        + [pl.BlockSpec((1, 4, L), lambda i: (i, 0, 0))],
        out_shape=[jax.ShapeDtypeStruct((T, D), BF16)] * 3
        + [jax.ShapeDtypeStruct((D, 256), F32)] * 4
        + [jax.ShapeDtypeStruct((PAIRS, 4, L), F32)],
        scratch_shapes=[
            pltpu.VMEM((T, D), BF16),
            pltpu.VMEM((2, T, L), F32),
            pltpu.VMEM((2, T, L), BF16),
            pltpu.VMEM((PAIR, L), F32),
        ],
        compiler_params=params(),
        cost_estimate=cost(1.2e10, 2.4e7),
        name="forward",
    )(place, tokens, kw, vw, q, g)


def merge_kernel(s0, s1, s2, s3, out):
    blocks = (s0, s1, s2, s3)
    top = functools.reduce(jnp.maximum, [b[:, 0:2, :] for b in blocks])
    total = jnp.zeros_like(top)
    inner = jnp.zeros_like(top)
    for b in blocks:
        factor = jnp.exp2(b[:, 0:2, :] - top)
        total += factor
        inner += b[:, 2:4, :] * factor
    out[:, 0:2, :] = top + jnp.log2(total)
    out[:, 2:4, :] = inner / total


def simple(kernel, ins, outs, name, scalars=None, scratch=(), moved=4e6, flops=1e6):
    specs = [pl.BlockSpec(memory_space=pltpu.VMEM)] * len(ins)
    several = isinstance(outs, list)
    shapes = [jax.ShapeDtypeStruct(o, F32) for o in (outs if several else [outs])]
    return pl.pallas_call(
        kernel,
        in_specs=([] if scalars is None else [SMEM]) + specs,
        out_shape=shapes if several else shapes[0],
        scratch_shapes=list(scratch),
        compiler_params=params(),
        cost_estimate=cost(flops, moved),
        name=name,
    )(*([] if scalars is None else [scalars]), *ins)


def reorder_kernel(order, normed, out):
    feature = lax.broadcasted_iota(jnp.int32, (D, D), 0)
    choose = jnp.where(feature == order[...], 1.0, 0.0).astype(BF16)
    out[...] = dot(normed[...], choose).astype(BF16).T


def reorder(order, normed):
    return pl.pallas_call(
        reorder_kernel,
        out_shape=jax.ShapeDtypeStruct((D, T), BF16),
        compiler_params=params(),
        cost_estimate=cost(2 * T * D * D, 3e6),
        name="reorder",
    )(order, normed)


def row_order(place):
    digits = [jnp.asarray(d, jnp.int32) for d in np.indices((4, 2, 4, 4, 10)).reshape(5, D)]
    z = (place[1] + digits[2]) % 4
    x = (place[0] + digits[3]) % 4
    owner = ((x * 4 + z) * 4 + digits[0]) * 2 + digits[1]
    return (owner * 10 + digits[4]).reshape(1, D)


def pair_cols(rows):
    return pl.BlockSpec((rows, PAIR), lambda i: (0, i))


def backward_kernel(nt, keys, vals, q, g, fin, out, q_out, s, pg, p, sg, kgrad, vgrad):
    keys_t = keys[...].T
    for j in range(2):
        head = slice(j * HD, (j + 1) * HD)
        for tile in range(L // 256):
            at = slice(tile * 256, (tile + 1) * 256)
            probs = jnp.exp2(nt_dot(keys[:, head], q[at, head]) * SCALE2 - fin[0, j : j + 1, at])
            p[j, :, at] = probs.astype(BF16)
            sg[j, :, at] = (probs * (nt_dot(vals[:, head], g[at, head]) - fin[0, 2 + j : 3 + j, at]) * SCALE).astype(BF16)
        query = dot(keys_t[head, :], sg[j]).T
        q_out[:, :, :, head] = query.reshape(2, 64, 8, HD)
        kgrad[:, head] = dot(sg[j], q[:, head]).astype(BF16)
        vgrad[:, head] = dot(p[j], g[:, head]).astype(BF16)
    out[:, 0:PAIR] = dot(nt[...], kgrad[...])
    out[:, PAIR:] = dot(nt[...], vgrad[...])


def backward(nt, keys, vals, q, g, fin):
    return pl.pallas_call(
        backward_kernel,
        grid=(PAIRS,),
        in_specs=[
            full((D, T)),
            pair_cols(T),
            pair_cols(T),
            pair_cols(L),
            pair_cols(L),
            pl.BlockSpec((1, 4, L), lambda i: (i, 0, 0)),
        ],
        out_specs=[
            pl.BlockSpec((D, 2 * PAIR), lambda i: (0, i)),
            pl.BlockSpec((2, 64, 8, PAIR), lambda i: (0, 0, 0, i)),
        ],
        out_shape=[jax.ShapeDtypeStruct((D, 2 * D), F32), jax.ShapeDtypeStruct((2, 64, 8, D), F32)],
        scratch_shapes=[
            pltpu.VMEM((2, T, L), F32),
            pltpu.VMEM((2, T, L), F32),
            pltpu.VMEM((2, T, L), BF16),
            pltpu.VMEM((2, T, L), BF16),
            pltpu.VMEM((T, PAIR), BF16),
            pltpu.VMEM((T, PAIR), BF16),
        ],
        compiler_params=params(),
        cost_estimate=cost(2e10, 3.0e7),
        name="backward",
    )(nt, keys, vals, q, g, fin)


def four(a0, a1, a2, a3):
    return (a0[...] + a2[...]) + (a1[...] + a3[...])


def exchange(chunks, axis):
    far = {k: shift(chunks[k], axis, k) for k in (2, 1, 3)}
    return [chunks[0], far[1], far[2], far[3]]


def second_kernel(rows, *outs):
    for k, out in enumerate(outs):
        out[...] = rows[k * 40 : (k + 1) * 40]


def third_kernel(a0, a1, a2, a3, *outs):
    rows = four(a0, a1, a2, a3)
    for k, out in enumerate(outs):
        out[0:10, :] = rows[k * 10 : (k + 1) * 10]
        out[10:16, :] = jnp.zeros((6, 2 * D), F32)


def last_kernel(a0, a1, a2, a3, key_rows, value_rows):
    rows = four(a0, a1, a2, a3)
    for i in range(PAIRS):
        cols = slice(i * PAIR, (i + 1) * PAIR)
        key_rows[:, cols] = rows[0:10, 2 * i * PAIR : (2 * i + 1) * PAIR]
        value_rows[:, cols] = rows[0:10, (2 * i + 1) * PAIR : (2 * i + 2) * PAIR]


def query_sum_kernel(parts, out):
    rows = parts[0]
    for k in range(1, 64):
        rows += parts[k]
    for k in range(16):
        out[k] = rows


def query_sum(parts):
    return simple(query_sum_kernel, [parts], (16, 8, D), "query_sum")


def place_query_kernel(place, own, other, *refs):
    out = refs[-1]

    @pl.when(pl.program_id(1) == 0)
    def _():
        out[...] = own[0]

    @pl.when(pl.program_id(1) == 1)
    def _():
        out[...] = other[0]


def place_query(place, hop, own, other, before=None):
    def spot(i, j, p):
        half = lax.rem(p[3] + j, 2)
        return half * 4 + lax.rem(p[0] + 4 - hop(i), 4), 0

    arrays = [own, other] + ([] if before is None else [before])
    return pl.pallas_call(
        place_query_kernel,
        grid_spec=pltpu.PrefetchScalarGridSpec(
            num_scalar_prefetch=1,
            grid=(own.shape[0], 2),
            in_specs=[pl.BlockSpec((1, 128, D), lambda i, j, p: (i, 0, 0))] * 2
            + [pl.BlockSpec(memory_space=pl.ANY)] * (len(arrays) - 2),
            out_specs=pl.BlockSpec((128, D), spot),
        ),
        out_shape=jax.ShapeDtypeStruct((L, D), F32),
        input_output_aliases={} if before is None else {3: 0},
        compiler_params=params(),
        cost_estimate=cost(1e6, 6e6),
        name="place_query",
    )(place, *arrays)


def spread(blocks):
    return lax.all_to_all(blocks, ("seq", "dp"), split_axis=0, concat_axis=0, axis_index_groups=CORE_GROUPS)


def numer_x_kernel(place, n0, n1, n2, n3, s0, s1, s2, s3, fin, z0, z1, z2, z3, total):
    at = pl.ds(pl.multiple_of(place[0] * 256, 256), 256)
    for h in range(H):
        rows = slice(h * HD, (h + 1) * HD)
        pair, j = h // 2, h % 2
        acc = jnp.zeros((HD, 256), F32)
        for n, s in ((n0, s0), (n1, s1), (n2, s2), (n3, s3)):
            acc += n[rows, :] * jnp.exp2(s[pair, j : j + 1, at] - fin[pair, j : j + 1, at])
        total[rows, :] = acc
    for k, out in enumerate((z0, z1, z2, z3)):
        spot = lax.rem(place[1] + k, 4)
        row = pl.multiple_of(lax.rem(spot, 2) * 640, 640)
        lane = pl.multiple_of(lax.div(spot, 2) * 128, 128)
        out[...] = total[pl.ds(row, 640), pl.ds(lane, 128)]


def numer_z_kernel(z0, z1, z2, z3, out):
    out[...] = four(z0, z1, z2, z3).T


def round_kernel(x, out):
    for k in range(2):
        rows = slice(k * 128, (k + 1) * 128)
        out[rows, 0:640] = x[2 * k].astype(BF16)
        out[rows, 640:1280] = x[2 * k + 1].astype(BF16)


def after(first, values):
    return lax.optimization_barrier((first, values))[1]


def on_device(tokens, queries, key_weight, value_weight, out_grad):
    seq, dp = lax.axis_index("seq"), lax.axis_index("dp")
    place = jnp.stack([seq // 4, seq % 4, dp // 2, dp % 2]).astype(jnp.int32)
    grad = out_grad[0]

    keys, vals, normed, n0, n1, n2, n3, stats = forward(place, tokens[0], key_weight, value_weight, queries, grad)
    near = exchange([stats] * 4, "x")
    nt = reorder(row_order(place), normed)
    near, nt, n1, n2, n3 = lax.optimization_barrier((near, nt, n1, n2, n3))
    group = simple(merge_kernel, near, (PAIRS, 4, L), "merge")
    blocks = exchange([group] * 4, "z")
    numer = exchange([n0, n1, n2, n3], "x")
    fin = simple(merge_kernel, blocks, (PAIRS, 4, L), "finish")

    terms, q_terms = backward(nt, keys, vals, queries, grad, fin)
    q_cores = lax.all_to_all(q_terms, "dp", split_axis=0, concat_axis=0, axis_index_groups=PAIR_GROUPS)
    q_sum = q_cores[0] + q_cores[1]
    q_parts = spread(q_sum)
    numer, near = after(q_sum, (numer, near))
    rows = lax.psum_scatter(after(numer, terms), "dp", scatter_dimension=0, tiled=True)
    own_query = lax.all_to_all(
        query_sum(q_parts), ("seq", "dp"), split_axis=0, concat_axis=0, axis_index_groups=PLANE_GROUPS
    ).reshape(128, D)

    zs = simple(
        numer_x_kernel,
        [*numer, *near, fin],
        [(640, 128)] * 4,
        "numer_x",
        scalars=place,
        scratch=[pltpu.VMEM((D, 256), F32)],
        moved=7e6,
    )
    share = simple(numer_z_kernel, exchange(zs, "z"), (128, 640), "numer_z")
    gathered = lax.all_gather(after(q_parts, share), "seq")
    right, left = shift(own_query, "x", 1), shift(own_query, "x", 3)
    rows = after((right, left), rows)
    far = shift(own_query, "x", 2)
    rows = exchange(simple(second_kernel, [rows], [(40, 2 * D)] * 4, "second"), "z")
    near_query = jnp.stack([own_query, right, left])
    query_grad = place_query(place, lambda i: i + i // 2, near_query, shift(near_query, "c", 1))
    rows = simple(third_kernel, after(query_grad, rows), [(16, 2 * D)] * 4, "third")
    far = after(rows[0], far).reshape(1, 128, D)
    rows = exchange(rows, "x")

    attended = pl.pallas_call(
        round_kernel,
        grid=(4,),
        in_specs=[pl.BlockSpec((4, 128, 640), lambda i: (i, 0, 0))],
        out_specs=pl.BlockSpec((256, D), lambda i: (i, 0)),
        out_shape=jax.ShapeDtypeStruct((L, D), BF16),
        compiler_params=params(),
        cost_estimate=cost(1e6, 8e6),
        name="round",
    )(gathered)
    far_other = after(attended, shift(far, "c", 1))
    query_grad = place_query(place, lambda i: 2, far, far_other, query_grad)
    key_rows, value_rows = simple(last_kernel, rows, [(10, D)] * 2, "last")
    return attended.reshape(1, L, D), query_grad, key_rows, value_rows


def solution(mesh):
    placed = (P("dp", "seq", None), P(), P(), P(), P("dp", None, None))
    return jax.shard_map(
        on_device,
        mesh=mesh,
        in_specs=placed,
        out_specs=(P("dp", None, None), P(), P(("seq", "dp"), None), P(("seq", "dp"), None)),
        check_vma=False,
    )
```
